512 devices in a mesh: dp: 64 (over z, x, core), tp: 8 (over y).
Axes of the slice: x: 4, y: 8, z: 8, core: 2. Of those that a mesh axis runs over, the one named last changes fastest.
Arguments:
- queries: bfloat16 [64, 4, 128, 576], P('dp', None, 'tp')
- new_latents: bfloat16 [64, 4, 576], P('dp'), may hold values from -6 to 6
- latent_cache: bfloat16 [64, 512, 576], P('dp')
- lengths: int32 [64], P('dp'), may hold values from 32 to 512, as said below
- slot_of: int32 [64], replicated, may hold values from 0 to 63, each once
- value_maps: bfloat16 [128, 512, 128], P('tp'), may hold values from -0.25 to 0.25
- out_proj: bfloat16 [16384, 7168], P('tp', 'dp'), may hold values from -0.046875 to 0.046875
- residual: bfloat16 [256, 7168], P(None, 'dp'), may hold values from -6 to 6
- norm_gain: bfloat16 [7168], P('dp'), may hold values from 0.25 to 1.75
- w_gate: bfloat16 [7168, 18432], P('dp', 'tp'), may hold values from -0.0625 to 0.0625
- w_up: bfloat16 [7168, 18432], P('dp', 'tp'), may hold values from -0.0625 to 0.0625
- w_down: bfloat16 [18432, 7168], P('tp', 'dp'), may hold values from -0.046875 to 0.046875
Outputs:
- layer_out: bfloat16 [256, 7168], P('tp', 'dp')
The draws below stay inside these ranges and needn't reach their ends.
Inputs may be any that keep to these rules, and one draw needn't show every extreme that they name: `lengths`: lengths differ widely between requests; some request has a full cache of 512 positions.
All inputs are finite; a program needn't handle non-finite values.
Results may differ from the reference program's by a relative error of at most 0.013.
Values may be sent and summed in bfloat16 or wider, within the bound.
No kernel may reach another device: no remote copies, remote signals or barrier semaphores. Data moves between devices by JAX's collectives and lax.ppermute only.
A program may use at most 64 MiB of HBM per device.

```python
import jax
import jax.numpy as jnp
from jax import lax

D = 7168
H = 128
LATN = 512
ROPE = 64
VDIM = 128
FF = 18432
LMAX = 512
STEPS = 4
LAT = 576
REQUESTS = 64
ROWS = 256


def latent_rows(key):
    return jax.random.normal(key, (REQUESTS, LMAX, LATN + ROPE), jnp.float32)


def draw_latent_cache(key, part):
    base = latent_rows(key)
    return base.astype(jnp.bfloat16)


def draw_queries(key, part):
    key = jax.random.fold_in(key, 2)
    values = 0.6 * jax.random.normal(key, (REQUESTS, STEPS, H, LATN + ROPE), jnp.float32)
    return values.astype(jnp.bfloat16)


def draw_lengths(key, part):
    key = jax.random.fold_in(key, 3)
    first_key, second_key = jax.random.split(key)
    halving = jax.random.randint(first_key, (REQUESTS,), 0, 4, jnp.int32)
    jitter = jax.random.randint(second_key, (REQUESTS,), 0, LMAX // 16, jnp.int32)
    spans = LMAX // jnp.left_shift(jnp.ones_like(halving), halving) - jitter
    return spans.at[0].set(LMAX).astype(jnp.int32)


def levels(own_key, shape, cuts, smallest, top_value):
    gain = 1.0
    for dim, shards_of in cuts:
        steps = jax.random.uniform(jax.random.fold_in(jax.random.fold_in(own_key, 6), dim), (shards_of,), jnp.float32, smallest / len(cuts), top_value / len(cuts))
        gain = gain * jnp.repeat(jnp.exp(steps), shape[dim] // shards_of).reshape((-1,) + (1,) * (len(shape) - 1 - dim))
    return gain


def centred(key, extent, scale, most, pieces=(), held_as=jnp.bfloat16):
    gain = levels(key, extent, pieces, -0.22, 0.18) if pieces else 1.0
    values = jax.random.normal(key, extent, jnp.float32) * scale * gain
    return jnp.minimum(jnp.maximum(values, -most), most).astype(held_as)


def setup_inputs(seed: int = 0) -> dict:
    keys = jax.random.split(jax.random.key(seed), 13)
    queries = draw_queries(jax.random.fold_in(keys[12], 71), 0)
    new_latents = centred(keys[1], (REQUESTS, STEPS, LAT), 1.0, 6.0, ((0, 64),))
    latent_cache = draw_latent_cache(jax.random.fold_in(keys[12], 71), 0)
    lengths = draw_lengths(jax.random.fold_in(keys[12], 71), 0)
    slot_of = jax.random.permutation(keys[4], REQUESTS).astype(jnp.int32)
    value_maps = centred(keys[5], (H, LATN, VDIM), LATN ** -0.5, 0.25, ((0, 8),))
    out_proj = centred(keys[6], (H * VDIM, D), (H * VDIM) ** -0.5, 0.046875, ((0, 8), (1, 64)))
    residual = centred(keys[7], (ROWS, D), 1.0, 6.0, ((1, 64),))
    norm_gain = jnp.clip(1.0 + 0.15 * jax.random.normal(keys[8], (D,), jnp.float32), 0.25, 1.75).astype(jnp.bfloat16)
    w_gate = centred(keys[9], (D, FF), D ** -0.5, 0.0625, ((0, 64), (1, 8)))
    w_up = centred(keys[10], (D, FF), D ** -0.5, 0.0625, ((0, 64), (1, 8)))
    w_down = centred(keys[11], (FF, D), FF ** -0.5, 0.046875, ((0, 8), (1, 64)))
    return dict(queries=queries, new_latents=new_latents, latent_cache=latent_cache, lengths=lengths, slot_of=slot_of, value_maps=value_maps, out_proj=out_proj, residual=residual, norm_gain=norm_gain, w_gate=w_gate, w_up=w_up, w_down=w_down)


score_scale = 192.0 ** (-0.5)
norm_eps = 1e-06

def attend(query_r, new_r, cache_r, valid_len):
    qf = query_r.astype(jnp.float32)
    score_cache = jnp.einsum('shc,lc->shl', qf, cache_r.astype(jnp.float32)) * score_scale
    score_new = jnp.einsum('shc,uc->shu', qf, new_r.astype(jnp.float32)) * score_scale
    keep_cache = (jnp.arange(LMAX, dtype=jnp.int32) < valid_len)[None, None, :]
    step_ids = jnp.arange(STEPS, dtype=jnp.int32)
    keep_new = (step_ids[None, :] <= step_ids[:, None])[:, None, :]
    row_max = jnp.maximum(lax.optimization_barrier(jnp.max(jnp.where(keep_cache, score_cache, -1e+30), axis=2, keepdims=True)), lax.optimization_barrier(jnp.max(jnp.where(keep_new, score_new, -1e+30), axis=2, keepdims=True)))
    weight_cache = jnp.where(keep_cache, jnp.exp(score_cache - row_max), 0.0)
    weight_new = jnp.where(keep_new, jnp.exp(score_new - row_max), 0.0)
    softmax_total = lax.optimization_barrier(jnp.sum(weight_cache, axis=2, keepdims=True)) + lax.optimization_barrier(jnp.sum(weight_new, axis=2, keepdims=True))
    prob_cache = (weight_cache / softmax_total).astype(jnp.bfloat16)
    prob_new = (weight_new / softmax_total).astype(jnp.bfloat16)
    context = jnp.einsum('shl,lc->shc', prob_cache.astype(jnp.float32), cache_r[:, :LATN].astype(jnp.float32))
    context = context + jnp.einsum('shu,uc->shc', prob_new.astype(jnp.float32), new_r[:, :LATN].astype(jnp.float32))
    return context.astype(jnp.bfloat16)

def reference(queries, new_latents, latent_cache, lengths, slot_of, value_maps, out_proj, residual, norm_gain, w_gate, w_up, w_down):
    context = lax.map(lambda items: attend(items[0], items[1], items[2], items[3]), (queries, new_latents, latent_cache, lengths))
    head_values = jnp.einsum('rshc,hcd->rshd', context.astype(jnp.float32), value_maps.astype(jnp.float32)).astype(jnp.bfloat16)
    head_values = head_values.reshape(REQUESTS, STEPS, H * VDIM)
    ordered = head_values[slot_of].reshape(ROWS, H * VDIM)
    hidden = residual.astype(jnp.float32) + jnp.dot(ordered, out_proj, preferred_element_type=jnp.float32)
    mean_square = lax.optimization_barrier(jnp.mean(hidden * hidden, axis=1, keepdims=True))
    normed = (hidden * lax.rsqrt(mean_square + norm_eps) * norm_gain.astype(jnp.float32)).astype(jnp.bfloat16)
    gate_sum = jnp.dot(normed, w_gate, preferred_element_type=jnp.float32)
    up_sum = jnp.dot(normed, w_up, preferred_element_type=jnp.float32)
    hidden_units = (jax.nn.silu(gate_sum) * up_sum).astype(jnp.bfloat16)
    down_term = jnp.dot(hidden_units, w_down, preferred_element_type=jnp.float32)
    return (hidden + down_term).astype(jnp.bfloat16)
```

```python
import jax
import jax.numpy as jnp
from jax import lax
from jax.sharding import Mesh
from jax.sharding import PartitionSpec as P

D = 7168

score_scale = 192.0 ** (-0.5)
norm_eps = 1e-06

AXES = ("z", "xh", "xl", "c", "y")
DP = ("z", "xh", "xl", "c")
BF = jnp.bfloat16
F32 = jnp.float32


def attention(queries, new_latents, latent_cache, lengths, value_maps):
    step_count = queries.shape[1]
    cache_len = latent_cache.shape[1]
    latent_width = value_maps.shape[1]
    score_cache = (
        jnp.einsum("rshc,rlc->rshl", queries, latent_cache, preferred_element_type=F32)
        * score_scale
    )
    score_new = (
        jnp.einsum("rshc,ruc->rshu", queries, new_latents, preferred_element_type=F32)
        * score_scale
    )
    position = jnp.arange(cache_len, dtype=jnp.int32)
    keep_cache = (position[None, :] < lengths[:, None])[:, None, None, :]
    step_ids = jnp.arange(step_count, dtype=jnp.int32)
    keep_new = (step_ids[None, :] <= step_ids[:, None])[None, :, None, :]
    row_max = jnp.maximum(
        jnp.max(jnp.where(keep_cache, score_cache, -1e30), axis=3, keepdims=True),
        jnp.max(jnp.where(keep_new, score_new, -1e30), axis=3, keepdims=True),
    )
    weight_cache = jnp.where(keep_cache, jnp.exp(score_cache - row_max), 0.0)
    weight_new = jnp.where(keep_new, jnp.exp(score_new - row_max), 0.0)
    softmax_total = jnp.sum(weight_cache, axis=3, keepdims=True) + jnp.sum(
        weight_new, axis=3, keepdims=True
    )
    prob_cache = (weight_cache / softmax_total).astype(BF)
    prob_new = (weight_new / softmax_total).astype(BF)
    context = jnp.einsum(
        "rshl,rlc->rshc",
        prob_cache,
        latent_cache[:, :, :latent_width],
        preferred_element_type=F32,
    )
    context = context + jnp.einsum(
        "rshu,ruc->rshc",
        prob_new,
        new_latents[:, :, :latent_width],
        preferred_element_type=F32,
    )
    context = context.astype(BF)
    head_values = jnp.einsum(
        "rshc,hcd->rshd", context, value_maps, preferred_element_type=F32
    ).astype(BF)
    return head_values.reshape(step_count, -1)


def swap(value, axis):
    return lax.ppermute(value, axis, [(0, 1), (1, 0)])


def exchange(blocks, axes):
    return lax.all_to_all(blocks, axes, 0, 0, tiled=True)


def gather(block, axes, count):
    return exchange(jnp.broadcast_to(block[None], (count,) + block.shape), axes)


def dot(a, b):
    return jnp.dot(a, b, preferred_element_type=F32)


def halves(weight, axis, index):
    size = weight.shape[axis] // 2
    keep = lax.dynamic_slice_in_dim(weight, index * size, size, axis)
    send = lax.dynamic_slice_in_dim(weight, (1 - index) * size, size, axis)
    return keep, send


def local(
    queries,
    new_latents,
    latent_cache,
    lengths,
    slot_of,
    value_maps,
    out_proj,
    residual,
    norm_gain,
    w_gate,
    w_up,
    w_down,
):
    xl, core, tp = lax.axis_index("xl"), lax.axis_index("c"), lax.axis_index("y")
    width = out_proj.shape[1]
    row_ids = jnp.arange(128, dtype=jnp.int32)
    out_ids = jnp.arange(256, dtype=jnp.int32)
    slot_rows = jnp.repeat(slot_of, 4) * 4 + out_ids % 4

    def placed(of_core):
        own = (row_ids // 4) * 8 + of_core * 4 + row_ids % 4
        return (slot_rows[:, None] == own[None, :]).astype(BF)

    mine, others = placed(core), placed(1 - core)
    block = lambda m: lax.dynamic_slice_in_dim(m, tp * 16, 16, 1)
    pick = lambda m: lax.dot_general(
        block(m), residual, (((0,), (0,)), ((), ())), preferred_element_type=F32
    ).astype(BF)
    head = pick(mine)
    other = swap(
        jnp.concatenate([pick(others), jnp.broadcast_to(norm_gain[None], (16, width))], axis=0), "c"
    )
    out_other = swap(out_proj, "c")

    head_values = attention(queries, new_latents, latent_cache, lengths, value_maps)

    gate_keep, gate_send = halves(w_gate, 1, xl)
    up_keep, up_send = halves(w_up, 1, xl)
    ff_own = jnp.concatenate([gate_keep, up_keep], axis=1)
    ff_next = swap(jnp.concatenate([gate_send, up_send], axis=1), "xl")
    ff_own_other = swap(ff_own, "c")
    ff_next_other = swap(ff_next, "c")
    down_own, down_send = halves(w_down, 0, xl)
    down_next = swap(down_send, "xl")
    down_own_other = swap(down_own, "c")
    down_next_other = swap(down_next, "c")

    rows = gather(head_values, ("z", "xh", "xl"), 32).reshape(128, -1)
    part = jnp.stack([dot(rows, out_proj), dot(rows, out_other)]).astype(BF)
    part = part.reshape(2, 8, 16, width).transpose(1, 0, 2, 3)
    attended = jnp.sum(exchange(part, "y").astype(F32), axis=0)
    start = jnp.stack([head, other[:16]]).astype(F32)
    gain = jnp.stack([norm_gain[None], other[16:17]]).astype(F32)
    hidden = start + attended
    squares = jnp.sum(hidden * hidden, axis=(0, 2))
    high = squares.astype(BF)
    low = (squares - high.astype(F32)).astype(BF)
    extra = jnp.stack([high, low], axis=1)
    extra = jnp.pad(extra[None], ((0, 1), (0, 0), (0, 128 - width - 2)))
    scaled = jnp.concatenate([(hidden * gain).astype(BF), extra], axis=2)

    full = gather(scaled, ("xl", "y"), 16).reshape(2, 8, 2, 16, 128)
    near = lax.dynamic_index_in_dim(full, xl, 0, False)
    far = lax.dynamic_index_in_dim(full, 1 - xl, 0, False)
    rows_of = lambda a, o: a[:, o, :, :width].reshape(128, width)
    ff = (
        dot(rows_of(near, 0), ff_own)
        + dot(rows_of(near, 1), ff_own_other)
        + dot(rows_of(far, 0), ff_next)
        + dot(rows_of(far, 1), ff_next_other)
    )
    sums = jnp.sum(full[:, :, 0, :, width : width + 2].astype(F32), axis=(0, 3)).reshape(128, 1)
    high = sums.astype(BF)
    low = (sums - high.astype(F32)).astype(BF)
    ff = jnp.concatenate([ff.astype(BF), high, low, jnp.zeros((128, 126), BF)], axis=1)
    total = jnp.sum(exchange(ff.reshape(16, 8, -1), ("z", "xh")).astype(F32), axis=0)
    half = w_gate.shape[1] // 2
    square_sums = total[:, 2 * half : 2 * half + 1] + total[:, 2 * half + 1 : 2 * half + 2]
    factor = lax.rsqrt(square_sums / D + norm_eps)
    units = (jax.nn.silu(total[:, :half] * factor) * (total[:, half : 2 * half] * factor)).astype(BF)

    units = gather(units, ("z", "xh"), 16).reshape(128, half)
    hidden_rows = lax.dynamic_update_slice_in_dim(
        jnp.zeros((2, 128, width), F32), hidden, tp * 16, 1
    )
    own = jnp.stack([dot(units, down_own), dot(units, down_own_other)]) + hidden_rows
    nxt = jnp.stack([dot(units, down_next), dot(units, down_next_other)])
    both = jnp.where(xl == 0, jnp.stack([own, nxt]), jnp.stack([nxt, own])).astype(BF)
    both = jnp.einsum("qr,xork->xoqk", mine, both, preferred_element_type=F32).astype(BF)
    both = both.reshape(2, 2, 8, 32, width).transpose(0, 2, 1, 3, 4).reshape(16, 2, 32, width)
    share = jnp.sum(exchange(both, ("xl", "y")).astype(F32), axis=0)
    return (share[0] + swap(share[1], "c")).astype(BF)


def solution(mesh):
    fine = Mesh(mesh.devices.reshape(8, 2, 2, 2, 8), AXES)
    placed = (
        P(DP, None, "y", None),
        P(DP, None, None),
        P(DP, None, None),
        P(DP),
        P(),
        P("y", None, None),
        P("y", DP),
        P(None, DP),
        P(DP),
        P(DP, "y"),
        P(DP, "y"),
        P("y", DP),
    )
    return jax.shard_map(
        local, mesh=fine, in_specs=placed, out_specs=P("y", DP), check_vma=False
    )
```

```python
import jax
import jax.numpy as jnp
from jax import lax
from jax.sharding import Mesh
from jax.sharding import PartitionSpec as P

D = 7168

score_scale = 192.0 ** (-0.5)
norm_eps = 1e-06

AXES = ("z", "xh", "xl", "c", "y")
DP = ("z", "xh", "xl", "c")
BF = jnp.bfloat16
F32 = jnp.float32


def attention(queries, new_latents, latent_cache, lengths, value_maps):
    step_count = queries.shape[1]
    cache_len = latent_cache.shape[1]
    latent_width = value_maps.shape[1]
    score_cache = (
        jnp.einsum("rshc,rlc->rshl", queries, latent_cache, preferred_element_type=F32)
        * score_scale
    )
    score_new = (
        jnp.einsum("rshc,ruc->rshu", queries, new_latents, preferred_element_type=F32)
        * score_scale
    )
    position = jnp.arange(cache_len, dtype=jnp.int32)
    keep_cache = (position[None, :] < lengths[:, None])[:, None, None, :]
    step_ids = jnp.arange(step_count, dtype=jnp.int32)
    keep_new = (step_ids[None, :] <= step_ids[:, None])[None, :, None, :]
    row_max = jnp.maximum(
        jnp.max(jnp.where(keep_cache, score_cache, -1e30), axis=3, keepdims=True),
        jnp.max(jnp.where(keep_new, score_new, -1e30), axis=3, keepdims=True),
    )
    weight_cache = jnp.where(keep_cache, jnp.exp(score_cache - row_max), 0.0)
    weight_new = jnp.where(keep_new, jnp.exp(score_new - row_max), 0.0)
    softmax_total = jnp.sum(weight_cache, axis=3, keepdims=True) + jnp.sum(
        weight_new, axis=3, keepdims=True
    )
    prob_cache = (weight_cache / softmax_total).astype(BF)
    prob_new = (weight_new / softmax_total).astype(BF)
    context = jnp.einsum(
        "rshl,rlc->rshc",
        prob_cache,
        latent_cache[:, :, :latent_width],
        preferred_element_type=F32,
    )
    context = context + jnp.einsum(
        "rshu,ruc->rshc",
        prob_new,
        new_latents[:, :, :latent_width],
        preferred_element_type=F32,
    )
    context = context.astype(BF)
    head_values = jnp.einsum(
        "rshc,hcd->rshd", context, value_maps, preferred_element_type=F32
    ).astype(BF)
    return head_values.reshape(step_count, -1)


def swap(value, axis):
    return lax.ppermute(value, axis, [(0, 1), (1, 0)])


def exchange(blocks, axes):
    return lax.all_to_all(blocks, axes, 0, 0, tiled=True)


def gather(block, axes, count):
    return exchange(jnp.broadcast_to(block[None], (count,) + block.shape), axes)


def dot(a, b):
    return jnp.dot(a, b, preferred_element_type=F32)


def local(
    queries,
    new_latents,
    latent_cache,
    lengths,
    slot_of,
    value_maps,
    out_proj,
    residual,
    norm_gain,
    w_gate,
    w_up,
    w_down,
):
    xh, xl = lax.axis_index("xh"), lax.axis_index("xl")
    core, tp = lax.axis_index("c"), lax.axis_index("y")
    width = out_proj.shape[1]
    row_ids = jnp.arange(128, dtype=jnp.int32)
    out_ids = jnp.arange(256, dtype=jnp.int32)
    slot_rows = jnp.repeat(slot_of, 4) * 4 + out_ids % 4

    def placed(of_core):
        own = (row_ids // 4) * 8 + of_core * 4 + row_ids % 4
        return (slot_rows[:, None] == own[None, :]).astype(BF)

    mine, others = placed(core), placed(1 - core)
    block = lambda m: lax.dynamic_slice_in_dim(m, tp * 16, 16, 1)
    pick = lambda m: lax.dot_general(
        block(m), residual, (((0,), (0,)), ((), ())), preferred_element_type=F32
    ).astype(BF)
    head = pick(mine)
    other = swap(
        jnp.concatenate([pick(others), jnp.broadcast_to(norm_gain[None], (16, width))], axis=0), "c"
    )
    out_other = swap(out_proj, "c")

    head_values = attention(queries, new_latents, latent_cache, lengths, value_maps)

    def piece(xh_to, xl_to):
        quarter = 2 * xh_to + xl_to
        cut = lambda w: lax.dynamic_slice_in_dim(w, quarter * size, size, 1)
        return jnp.concatenate([cut(w_gate), cut(w_up)], axis=1)

    def spread(mine, for_xh, for_xl, for_both):
        from_xl = swap(jnp.stack([for_xl, for_both]), "xl")
        from_xh = swap(jnp.stack([for_xh, from_xl[1]]), "xh")
        held = jnp.concatenate([mine[None], from_xl[:1], from_xh], axis=0)
        return held, swap(held, "c")

    size = w_gate.shape[1] // 4
    ff_own, ff_other = spread(
        piece(xh, xl), piece(1 - xh, xl), piece(xh, 1 - xl), piece(1 - xh, 1 - xl)
    )

    def rows_piece(xh_to, xl_to):
        return lax.dynamic_slice_in_dim(w_down, (2 * xh_to + xl_to) * size, size, 0)

    down_own, down_other = spread(
        rows_piece(xh, xl), rows_piece(1 - xh, xl), rows_piece(xh, 1 - xl), rows_piece(1 - xh, 1 - xl)
    )

    rows = gather(head_values, ("z", "xh", "xl"), 32).reshape(128, -1)
    part = jnp.stack([dot(rows, out_proj), dot(rows, out_other)]).astype(BF)
    part = part.reshape(2, 8, 16, width).transpose(1, 0, 2, 3)
    attended = jnp.sum(exchange(part, "y").astype(F32), axis=0)
    start = jnp.stack([head, other[:16]]).astype(F32)
    gain = jnp.stack([norm_gain[None], other[16:17]]).astype(F32)
    hidden = start + attended
    squares = jnp.sum(hidden * hidden, axis=(0, 2))
    high = squares.astype(BF)
    low = (squares - high.astype(F32)).astype(BF)
    extra = jnp.stack([high, low], axis=1)
    extra = jnp.pad(extra[None], ((0, 1), (0, 0), (0, 128 - width - 2)))
    scaled = jnp.concatenate([(hidden * gain).astype(BF), extra], axis=2)

    full = gather(scaled, ("xh", "xl", "y"), 32).reshape(4, 8, 2, 16, 128)
    order = [2 * xh + xl, 2 * xh + 1 - xl, 2 * (1 - xh) + xl, 2 * (1 - xh) + 1 - xl]
    ff = jnp.zeros((128, 2 * size), F32)
    for i in range(4):
        held = lax.dynamic_index_in_dim(full, order[i], 0, False)
        ff = ff + dot(held[:, 0, :, :width].reshape(128, width), ff_own[i])
        ff = ff + dot(held[:, 1, :, :width].reshape(128, width), ff_other[i])
    sums = jnp.sum(full[:, :, 0, :, width : width + 2].astype(F32), axis=(0, 3)).reshape(128, 1)
    high = sums.astype(BF)
    low = (sums - high.astype(F32)).astype(BF)
    ff = jnp.concatenate([ff.astype(BF), high, low, jnp.zeros((128, 126), BF)], axis=1)
    total = jnp.sum(exchange(ff.reshape(8, 16, -1), "z").astype(F32), axis=0)
    square_sums = total[:, 2 * size : 2 * size + 1] + total[:, 2 * size + 1 : 2 * size + 2]
    factor = lax.rsqrt(square_sums / D + norm_eps)
    units = (jax.nn.silu(total[:, :size] * factor) * (total[:, size : 2 * size] * factor)).astype(BF)

    units = gather(units, "z", 8).reshape(128, size)
    product = lambda w: jnp.einsum("rk,bkn->brn", units, w, preferred_element_type=F32)
    hidden_rows = lax.dynamic_update_slice_in_dim(
        jnp.zeros((2, 128, width), F32), hidden, tp * 16, 1
    )
    at_own = lambda a, o: jnp.concatenate([a[:1] + hidden_rows[o], a[1:]], axis=0).astype(BF)
    for_own = at_own(product(down_own), 0)
    for_other = swap(at_own(product(down_other), 1), "c")
    ranks = jnp.stack([jnp.argmax(jnp.stack(order) == i) for i in range(4)])
    place = lambda m, a: jnp.einsum("qr,xrk->xqk", m, a, preferred_element_type=F32)
    both = (place(mine, for_own) + place(others, for_other)).astype(BF)
    both = jnp.take(both, ranks, axis=0).reshape(32, 32, width)
    return jnp.sum(exchange(both, ("xh", "xl", "y")).astype(F32), axis=0).astype(BF)


def solution(mesh):
    fine = Mesh(mesh.devices.reshape(8, 2, 2, 2, 8), AXES)
    placed = (
        P(DP, None, "y", None),
        P(DP, None, None),
        P(DP, None, None),
        P(DP),
        P(),
        P("y", None, None),
        P("y", DP),
        P(None, DP),
        P(DP),
        P(DP, "y"),
        P(DP, "y"),
        P("y", DP),
    )
    return jax.shard_map(
        local, mesh=fine, in_specs=placed, out_specs=P("y", DP), check_vma=False
    )
```

```python
import jax
import jax.numpy as jnp
from jax import lax
from jax.experimental import pallas as pl
from jax.experimental.pallas import tpu as pltpu
from jax.sharding import Mesh
from jax.sharding import PartitionSpec as P

D = 7168
WIDTH = 112
SIZE = 576

PACK = 14 * 128

score_scale = 192.0 ** (-0.5)
norm_eps = 1e-06

AXES = ("z", "x", "c", "y")
DP = ("z", "x", "c")
BF = jnp.bfloat16
F32 = jnp.float32
VMEM = pl.BlockSpec(memory_space=pltpu.VMEM)
SMEM = pl.BlockSpec(memory_space=pltpu.SMEM)
HBM = pl.BlockSpec(memory_space=pltpu.HBM)


def call(kernel, in_specs, outs, scratch=(), flops=0, moved=0, limit=24):
    many = isinstance(outs, (list, tuple))
    return pl.pallas_call(
        kernel,
        in_specs=in_specs,
        out_specs=[VMEM] * len(outs) if many else VMEM,
        out_shape=list(outs) if many else outs,
        scratch_shapes=list(scratch),
        compiler_params=pltpu.CompilerParams(vmem_limit_bytes=limit * 1024 * 1024),
        cost_estimate=pl.CostEstimate(flops=flops, bytes_accessed=moved, transcendentals=0),
    )


def shape(dims, dtype=BF):
    return jax.ShapeDtypeStruct(dims, dtype)


def dot(a, b):
    return jnp.dot(a, b, preferred_element_type=F32)


def attention_kernel(len_ref, q_ref, new_ref, cache_ref, maps_ref, out_ref, q_in, cache, maps, ctx, heads, sems):
    fetches = [
        pltpu.make_async_copy(src, dst, sems.at[i])
        for i, (src, dst) in enumerate(((q_ref, q_in), (cache_ref, cache), (maps_ref, maps)))
    ]
    for fetch in fetches:
        fetch.start()
    new = new_ref[...]
    nt = (((1,), (1,)), ((), ()))
    fetches[0].wait()
    q = q_in[...]
    fresh = lax.dot_general(q, new, nt, preferred_element_type=F32) * score_scale
    fetches[1].wait()
    score = dot(q, cache[...]) * score_scale
    keep = lax.broadcasted_iota(jnp.int32, score.shape, 1) < len_ref[0]
    step = lax.broadcasted_iota(jnp.int32, fresh.shape, 0) // 16
    keep_new = lax.broadcasted_iota(jnp.int32, fresh.shape, 1) <= step
    score = jnp.where(keep, score, -1e30)
    fresh = jnp.where(keep_new, fresh, -1e30)
    top = jnp.maximum(
        jnp.max(score, axis=1, keepdims=True), jnp.max(fresh, axis=1, keepdims=True)
    )
    weight = jnp.where(keep, jnp.exp(score - top), 0.0)
    weight_new = jnp.where(keep_new, jnp.exp(fresh - top), 0.0)
    total = jnp.sum(weight, axis=1, keepdims=True) + jnp.sum(weight_new, axis=1, keepdims=True)
    prob = (weight / total).astype(BF)
    prob_new = (weight_new / total).astype(BF)
    context = lax.dot_general(prob, cache[:512, :], nt, preferred_element_type=F32)
    context = (context + dot(prob_new, new[:, :512])).astype(BF).astype(F32)
    for n in range(4):
        ctx[n] = context[:, n * 128 : (n + 1) * 128]
    fetches[2].wait()
    for h in range(16):
        rows = jnp.concatenate([ctx[n, pl.ds(h, 4, stride=16), :] for n in range(4)], axis=1).astype(BF)
        k, place = h // 4, h % 4
        heads[k * 4 : k * 4 + 4, place * 128 : place * 128 + 128] = dot(rows, maps[h])
    block = heads[...].astype(BF)
    for i in range(32):
        out_ref[i] = block


def pack_kernel(x_ref, gate_ref, up_ref, down_ref, *outs):
    pad = jnp.zeros((WIDTH, PACK - 3 * SIZE), BF)
    for r, out_ref in enumerate(outs):
        for q in range(4):

            @pl.when((x_ref[0] ^ r) == q)
            def _(out_ref=out_ref, q=q):
                cut = slice(q * SIZE, (q + 1) * SIZE)
                out_ref[...] = jnp.concatenate(
                    [gate_ref[:, cut], up_ref[:, cut], down_ref[:, cut], pad], axis=1
                )


def out_kernel(x_ref, own_ref, other_ref, out_ref, wide):
    for n in range(4):
        wide[n] = x_ref[:, :, n * 128 : (n + 1) * 128].reshape(512, 128).astype(F32)
    pad = jnp.zeros((128 - WIDTH, 512), BF)
    total = jnp.zeros((128, 256), F32)
    for k in range(4):
        rows = []
        for t in range(4):
            tiles = [wide[n, pl.ds(k * 4 + t, 32, stride=16), :] for n in range(4)]
            rows.append(jnp.concatenate(tiles, axis=1).astype(BF))
        cut = slice(k * 512, (k + 1) * 512)
        w = jnp.concatenate([own_ref[:, cut], pad, other_ref[:, cut], pad], axis=0)
        total = total + lax.dot_general(
            jnp.concatenate(rows, axis=0), w, (((1,), (1,)), ((), ())), preferred_element_type=F32
        )
    total = total.astype(BF)
    for y in range(8):
        part = total[y * 16 : y * 16 + 16]
        out_ref[y, 0:16, :] = part[:, :WIDTH]
        out_ref[y, 16:32, :] = part[:, 128 : 128 + WIDTH]


def norm_kernel(part_ref, pick_ref, own_ref, other_ref, out_ref, hidden_ref):
    attended = part_ref[0].astype(F32)
    for i in range(1, 8):
        attended = attended + part_ref[i].astype(F32)
    nt = (((1,), (1,)), ((), ()))
    pick = pick_ref[...]
    unit = (lax.broadcasted_iota(jnp.int32, (16, 128), 1) == 0).astype(F32).astype(BF)
    picked = lambda ref: lax.dot_general(pick, ref[:, :256], nt, preferred_element_type=F32)
    gains = lambda ref: lax.dot_general(unit, ref[:, 256:], nt, preferred_element_type=F32)
    hidden = attended + jnp.concatenate([picked(own_ref), picked(other_ref)], axis=0)
    gain = jnp.concatenate([gains(own_ref), gains(other_ref)], axis=0)
    squares = jnp.sum(hidden * hidden, axis=1, keepdims=True)
    squares = squares[0:16] + squares[16:32]
    high = squares.astype(BF).astype(F32)
    low = squares - high
    none = jnp.zeros((32, 128 - WIDTH), F32)
    scaled = jnp.concatenate([hidden * gain, none], axis=1)
    lane = lax.broadcasted_iota(jnp.int32, (32, 128), 1)
    first = lax.broadcasted_iota(jnp.int32, (32, 128), 0) < 16
    twice = lambda a: jnp.concatenate([a, a], axis=0)
    scaled = jnp.where(first & (lane == WIDTH), twice(high), scaled)
    scaled = jnp.where(first & (lane == WIDTH + 1), twice(low), scaled).astype(BF)
    hidden_ref[...] = jnp.concatenate([hidden, none], axis=1)
    for i in range(32):
        out_ref[i] = scaled


def gate_kernel(x_ref, full_ref, *refs):
    own_refs, other_refs, out_ref = refs[:4], refs[4:8], refs[8]
    lane = lax.broadcasted_iota(jnp.int32, (128, 128), 1)
    valid = lane < WIDTH
    none = jnp.zeros((128 - WIDTH, 384), BF)
    held, squares = [], jnp.zeros((128, 1), F32)
    for r in range(4):
        block = full_ref[pl.ds((x_ref[0] ^ r) * 8, 8)]
        own = block[:, 0:16, :].reshape(128, 128)
        other = block[:, 16:32, :].reshape(128, 128)
        sums = jnp.where((lane >= WIDTH) & (lane < WIDTH + 2), own.astype(F32), 0.0)
        squares = squares + jnp.sum(sums, axis=1, keepdims=True)
        zero = jnp.zeros((128, 128), BF)
        held.append(
            jnp.concatenate([jnp.where(valid, own, zero), jnp.where(valid, other, zero)], axis=1)
        )
    for n in range(0, 1152, 384):
        total = jnp.zeros((128, 384), F32)
        for r, w in enumerate(own_refs):
            both = [w[:, n : n + 384], none, other_refs[r][:, n : n + 384], none]
            total = total + dot(held[r], jnp.concatenate(both, axis=0))
        out_ref[:, :, n : n + 384] = total.astype(BF).reshape(8, 16, 384)
    high = squares.astype(BF).astype(F32)
    last = jnp.where(lane == 0, high, jnp.where(lane == 1, squares - high, 0.0))
    out_ref[:, :, 1152:1280] = last.astype(BF).reshape(8, 16, 128)


def units_kernel(part_ref, out_ref):
    total = part_ref[0].astype(F32)
    for i in range(1, 8):
        total = total + part_ref[i].astype(F32)
    squares = total[:, 2 * SIZE : 2 * SIZE + 1] + total[:, 2 * SIZE + 1 : 2 * SIZE + 2]
    factor = lax.rsqrt(squares / D + norm_eps)
    gate = total[:, :SIZE] * factor
    up = total[:, SIZE : 2 * SIZE] * factor
    units = (gate * jax.nn.sigmoid(gate) * up).astype(BF)
    for i in range(8):
        out_ref[i] = units


def down_kernel(
    x_ref, y_ref, own_ref, other_ref, w0, w1, w2, w3, hidden_ref, across_ref, place_ref, out_ref, total
):
    units = jnp.concatenate(
        [own_ref[...].reshape(128, SIZE), other_ref[...].reshape(128, SIZE)], axis=0
    )
    place = place_ref[...]
    none = jnp.zeros((128 - WIDTH, SIZE), BF)
    for r, w in enumerate((w0, w1, w2, w3)):
        part = lax.dot_general(
            units, jnp.concatenate([w[:, 2 * SIZE : 3 * SIZE], none], axis=0), (((1,), (1,)), ((), ())), preferred_element_type=F32
        )
        if r == 0:
            total[...] = part
            at = pl.multiple_of(y_ref[0] * 16, 16)
            total[pl.ds(at, 16), :] += hidden_ref[0:16, :]
            total[pl.ds(128 + at, 16), :] += across_ref[...]
            part = total[...]
        rows = dot(place, part.astype(BF)).astype(BF)
        out_ref[pl.ds((x_ref[0] ^ r) * 8, 8)] = rows[:, :WIDTH].reshape(8, 32, WIDTH)


def swap(value, axis="c"):
    return lax.ppermute(value, axis, [(0, 1), (1, 0)])


def exchange(blocks, axes):
    return lax.all_to_all(blocks, axes, 0, 0, tiled=True)


def local(
    queries,
    new_latents,
    latent_cache,
    lengths,
    slot_of,
    value_maps,
    out_proj,
    residual,
    norm_gain,
    w_gate,
    w_up,
    w_down,
):
    x, core, tp = lax.axis_index("x"), lax.axis_index("c"), lax.axis_index("y")
    xs, ys = x[None].astype(jnp.int32), tp[None].astype(jnp.int32)

    blocks = call(
        attention_kernel,
        [SMEM, HBM, VMEM, HBM, HBM],
        shape((32, 16, 512)),
        [
            pltpu.VMEM((64, 576), BF),
            pltpu.VMEM((576, 512), BF),
            pltpu.VMEM((16, 512, 128), BF),
            pltpu.VMEM((4, 64, 128), F32),
            pltpu.VMEM((16, 512), F32),
            pltpu.SemaphoreType.DMA((3,)),
        ],
        200_000_000,
        4_000_000,
        56,
    )(lengths, queries.reshape(64, -1), new_latents[0], latent_cache[0].T, value_maps)
    blocks, out_proj, slot_of, residual, norm_gain, w_gate, w_up, w_down = lax.optimization_barrier(
        (blocks, out_proj.T, slot_of, residual.T, norm_gain, w_gate, w_up, w_down.T)
    )
    rows = exchange(blocks, ("z", "x"))
    gains = jnp.broadcast_to(norm_gain[:, None], (WIDTH, 128))
    carry = jnp.concatenate([out_proj, residual, gains], axis=1)
    carry_other = swap(carry)
    tail, tail_other = carry[:, 2048:], carry_other[:, 2048:]

    ids = jnp.arange(128, dtype=jnp.int32)
    request_rows = jnp.repeat(slot_of, 4) * 4 + jnp.arange(256, dtype=jnp.int32) % 4
    held_rows = lambda of_core, own: (own % 32) * 8 + of_core * 4 + own // 32
    part_ids = tp * 16 + jnp.arange(16, dtype=jnp.int32)
    pick = (held_rows(core, part_ids)[:, None] == request_rows[None, :]).astype(BF)
    both_rows = jnp.concatenate([held_rows(core, ids), held_rows(1 - core, ids)])
    place = (request_rows[:, None] == both_rows[None, :]).astype(BF)

    packed = call(
        pack_kernel, [SMEM, VMEM, VMEM, VMEM], [shape((WIDTH, PACK))] * 4, (), 0, 3_200_000
    )(xs, w_gate, w_up, w_down)
    weights = [packed[0]] + [
        lax.ppermute(packed[r], "x", [(i, i ^ r) for i in range(4)]) for r in (1, 2, 3)
    ]
    part = call(
        out_kernel,
        [VMEM] * 3,
        shape((8, 32, WIDTH)),
        [pltpu.VMEM((4, 512, 128), F32)],
        300_000_000,
        1_600_000,
    )(rows, out_proj, carry_other)
    scaled, hidden = call(
        norm_kernel, [VMEM] * 4, [shape((32, 32, 128)), shape((32, 128), F32)], (), 0, 400_000
    )(exchange(part, "y"), pick, tail, tail_other)
    scaled, *weights = lax.optimization_barrier((scaled, *weights))
    others = [swap(w) for w in weights]
    part = call(
        gate_kernel, [SMEM] + [VMEM] * 9, shape((8, 16, 1280)), (), 300_000_000, 2_800_000
    )(xs, exchange(scaled, ("x", "y")), *weights, *others)
    units = call(units_kernel, [VMEM], shape((8, 16, SIZE)), (), 0, 500_000)(exchange(part, "z"))
    units, hidden = lax.optimization_barrier((units, hidden))
    across = swap(hidden[16:])
    units = exchange(units, "z")
    part = call(
        down_kernel,
        [SMEM] * 2 + [VMEM] * 9,
        shape((32, 32, WIDTH)),
        [pltpu.VMEM((256, 128), F32)],
        200_000_000,
        1_600_000,
    )(xs, ys, units, swap(units), *weights, hidden, across, place)
    return jnp.sum(exchange(part, ("x", "y")).astype(F32), axis=0).astype(BF)


def solution(mesh):
    fine = Mesh(mesh.devices.reshape(8, 4, 2, 8), AXES)
    specs = (
        P(DP, None, "y", None),
        P(DP, None, None),
        P(DP, None, None),
        P(DP),
        P(),
        P("y", None, None),
        P("y", DP),
        P(None, DP),
        P(DP),
        P(DP, "y"),
        P(DP, "y"),
        P("y", DP),
    )
    return jax.shard_map(
        local, mesh=fine, in_specs=specs, out_specs=P("y", DP), check_vma=False
    )
```

```python
import jax
import jax.numpy as jnp
from jax import lax
from jax.experimental import pallas as pl
from jax.experimental.pallas import tpu as pltpu
from jax.sharding import Mesh
from jax.sharding import PartitionSpec as P

D = 7168
WIDTH = 112
SIZE = 576
DOWN = 5 * 128

score_scale = 192.0 ** (-0.5)
norm_eps = 1e-06

AXES = ("z", "xh", "xl", "c", "y")
DP = ("z", "xh", "xl", "c")
BF = jnp.bfloat16
F32 = jnp.float32
VMEM = pl.BlockSpec(memory_space=pltpu.VMEM)
SMEM = pl.BlockSpec(memory_space=pltpu.SMEM)
HBM = pl.BlockSpec(memory_space=pltpu.HBM)


def call(kernel, in_specs, outs, scratch=(), flops=0, moved=0, limit=24):
    many = isinstance(outs, (list, tuple))
    return pl.pallas_call(
        kernel,
        in_specs=in_specs,
        out_specs=[VMEM] * len(outs) if many else VMEM,
        out_shape=list(outs) if many else outs,
        scratch_shapes=list(scratch),
        compiler_params=pltpu.CompilerParams(vmem_limit_bytes=limit * 1024 * 1024),
        cost_estimate=pl.CostEstimate(flops=flops, bytes_accessed=moved, transcendentals=0),
    )


def shape(dims, dtype=BF):
    return jax.ShapeDtypeStruct(dims, dtype)


def dot(a, b):
    return jnp.dot(a, b, preferred_element_type=F32)


def attention_kernel(len_ref, q_ref, new_ref, cache_ref, maps_ref, out_ref, q_in, cache, maps, ctx, heads, sems):
    fetches = [
        pltpu.make_async_copy(src, dst, sems.at[i])
        for i, (src, dst) in enumerate(((q_ref, q_in), (cache_ref, cache), (maps_ref, maps)))
    ]
    for fetch in fetches:
        fetch.start()
    new = new_ref[...]
    nt = (((1,), (1,)), ((), ()))
    fetches[0].wait()
    q = q_in[...]
    fresh = lax.dot_general(q, new, nt, preferred_element_type=F32) * score_scale
    fetches[1].wait()
    score = dot(q, cache[...]) * score_scale
    keep = lax.broadcasted_iota(jnp.int32, score.shape, 1) < len_ref[0]
    step = lax.broadcasted_iota(jnp.int32, fresh.shape, 0) // 16
    keep_new = lax.broadcasted_iota(jnp.int32, fresh.shape, 1) <= step
    score = jnp.where(keep, score, -1e30)
    fresh = jnp.where(keep_new, fresh, -1e30)
    top = jnp.maximum(
        jnp.max(score, axis=1, keepdims=True), jnp.max(fresh, axis=1, keepdims=True)
    )
    weight = jnp.where(keep, jnp.exp(score - top), 0.0)
    weight_new = jnp.where(keep_new, jnp.exp(fresh - top), 0.0)
    total = jnp.sum(weight, axis=1, keepdims=True) + jnp.sum(weight_new, axis=1, keepdims=True)
    prob = (weight / total).astype(BF)
    prob_new = (weight_new / total).astype(BF)
    context = lax.dot_general(prob, cache[:512, :], nt, preferred_element_type=F32)
    context = (context + dot(prob_new, new[:, :512])).astype(BF).astype(F32)
    for n in range(4):
        ctx[n] = context[:, n * 128 : (n + 1) * 128]
    fetches[2].wait()
    for h in range(16):
        rows = jnp.concatenate([ctx[n, pl.ds(h, 4, stride=16), :] for n in range(4)], axis=1).astype(BF)
        k, place = h // 4, h % 4
        heads[k * 4 : k * 4 + 4, place * 128 : place * 128 + 128] = dot(rows, maps[h])
    block = heads[...].astype(BF)
    for i in range(32):
        out_ref[i] = block


def pack_kernel(xh_ref, xl_ref, gate_ref, up_ref, down_ref, ff0, ff1, ff2, ff3, fd_ref, send_fd_ref):
    cuts = [slice(i * SIZE, (i + 1) * SIZE) for i in range(4)]
    pad = jnp.zeros((WIDTH, DOWN - SIZE), BF)
    for i, cut in enumerate(cuts):
        block = jnp.concatenate([gate_ref[:, cut], up_ref[:, cut]], axis=1)
        for r, out_ref in enumerate((ff0, ff1, ff2, ff3)):
            target = 2 * (xl_ref[0] ^ (r & 1)) + (xh_ref[0] ^ (r >> 1))

            @pl.when(target == i)
            def _(out_ref=out_ref, block=block):
                out_ref[...] = block

    for half in range(2):
        both = [down_ref[:, cuts[2 * half]], pad, down_ref[:, cuts[2 * half + 1]], pad]
        both = jnp.concatenate(both, axis=1)

        @pl.when(xl_ref[0] == half)
        def _(both=both):
            fd_ref[...] = both

        @pl.when(xl_ref[0] != half)
        def _(both=both):
            send_fd_ref[...] = both


def rows_kernel(core_ref, y_ref, slot_ref, pick_ref, place_ref):
    iota = lambda dims, axis: lax.broadcasted_iota(jnp.int32, dims, axis)
    slot = slot_ref[...].astype(F32)
    col = iota((256, 256), 1)
    core = jnp.where(col < 128, core_ref[0], 1 - core_ref[0])
    held = (col & 31) * 8 + core * 4 + ((col >> 5) & 3)
    spread = (iota((256, 64), 0) >> 2) == iota((256, 64), 1)
    of_row = jnp.sum(jnp.where(spread, slot, 0.0), axis=1, keepdims=True).astype(jnp.int32)
    place = (of_row * 4 + (iota((256, 256), 0) & 3)) == held
    place_ref[...] = jnp.where(place, 1.0, 0.0).astype(BF)
    across = jnp.where((iota((64, 256), 1) >> 2) == iota((64, 256), 0), 1.0, 0.0).astype(BF)
    of_col = dot(jnp.broadcast_to(slot, (16, 64)).astype(BF), across).astype(jnp.int32)
    own = iota((16, 256), 0) + y_ref[0] * 16
    held = (own & 31) * 8 + core_ref[0] * 4 + (own >> 5)
    pick_ref[...] = jnp.where(of_col * 4 + (iota((16, 256), 1) & 3) == held, 1.0, 0.0).astype(BF)


def out_kernel(x_ref, own_ref, other_ref, out_ref, wide):
    for n in range(4):
        wide[n] = x_ref[:, :, n * 128 : (n + 1) * 128].reshape(512, 128).astype(F32)
    pad = jnp.zeros((128 - WIDTH, 512), BF)
    total = jnp.zeros((128, 256), F32)
    for k in range(4):
        rows = []
        for t in range(4):
            tiles = [wide[n, pl.ds(k * 4 + t, 32, stride=16), :] for n in range(4)]
            rows.append(jnp.concatenate(tiles, axis=1).astype(BF))
        cut = slice(k * 512, (k + 1) * 512)
        w = jnp.concatenate([own_ref[:, cut], pad, other_ref[:, cut], pad], axis=0)
        total = total + lax.dot_general(
            jnp.concatenate(rows, axis=0), w, (((1,), (1,)), ((), ())), preferred_element_type=F32
        )
    total = total.astype(BF)
    for y in range(8):
        part = total[y * 16 : y * 16 + 16]
        out_ref[y, 0:16, :] = part[:, :128]
        out_ref[y, 16:32, :] = part[:, 128:]


def norm_kernel(part_ref, pick_ref, own_ref, other_ref, out_ref, hidden_ref):
    attended = part_ref[0].astype(F32)
    for i in range(1, 8):
        attended = attended + part_ref[i].astype(F32)
    attended = attended[:, :WIDTH]
    nt = (((1,), (1,)), ((), ()))
    pick = pick_ref[...]
    unit = (lax.broadcasted_iota(jnp.int32, (16, 128), 1) == 0).astype(F32).astype(BF)
    picked = lambda ref: lax.dot_general(pick, ref[:, :256], nt, preferred_element_type=F32)
    gains = lambda ref: lax.dot_general(unit, ref[:, 256:], nt, preferred_element_type=F32)
    hidden = attended + jnp.concatenate([picked(own_ref), picked(other_ref)], axis=0)
    gain = jnp.concatenate([gains(own_ref), gains(other_ref)], axis=0)
    squares = jnp.sum(hidden * hidden, axis=1, keepdims=True)
    squares = squares[0:16] + squares[16:32]
    none = jnp.zeros((32, 128 - WIDTH), F32)
    scaled = jnp.concatenate([hidden * gain, none], axis=1)
    lane = lax.broadcasted_iota(jnp.int32, (32, 128), 1)
    first = lax.broadcasted_iota(jnp.int32, (32, 128), 0) < 16
    high = squares.astype(BF).astype(F32)
    twice = lambda a: jnp.concatenate([a, a], axis=0)
    scaled = jnp.where(first & (lane == WIDTH), twice(high), scaled)
    scaled = jnp.where(first & (lane == WIDTH + 1), twice(squares - high), scaled).astype(BF)
    hidden_ref[...] = jnp.concatenate([hidden, none], axis=1)
    for i in range(32):
        out_ref[i] = scaled


def gate_kernel(xh_ref, xl_ref, full_ref, *refs):
    own_refs, other_refs, out_ref = refs[:4], refs[4:8], refs[8]
    lane = lax.broadcasted_iota(jnp.int32, (128, 128), 1)
    valid = lane < WIDTH
    none = jnp.zeros((128 - WIDTH, 384), BF)
    zero = jnp.zeros((128, 128), BF)
    held, squares = [], jnp.zeros((128, 1), F32)
    for r in range(4):
        x = 2 * (xh_ref[0] ^ (r >> 1)) + (xl_ref[0] ^ (r & 1))
        block = full_ref[pl.ds(x * 8, 8)]
        own = block[:, 0:16, :].reshape(128, 128)
        other = block[:, 16:32, :].reshape(128, 128)
        sums = jnp.where((lane == WIDTH) | (lane == WIDTH + 1), own.astype(F32), 0.0)
        squares = squares + jnp.sum(sums, axis=1, keepdims=True)
        both = [jnp.where(valid, own, zero), jnp.where(valid, other, zero)]
        held.append(jnp.concatenate(both, axis=1))
    for n in range(0, 2 * SIZE, 384):
        total = jnp.zeros((128, 384), F32)
        for r in range(4):
            both = [own_refs[r][:, n : n + 384], none, other_refs[r][:, n : n + 384], none]
            total = total + dot(held[r], jnp.concatenate(both, axis=0))
        out_ref[:, :, n : n + 384] = total.astype(BF).reshape(8, 16, 384)
    high = squares.astype(BF).astype(F32)
    last = jnp.where(lane == 0, high, jnp.where(lane == 1, squares - high, 0.0))
    out_ref[:, :, 1152:1280] = last.astype(BF).reshape(8, 16, 128)


def units_kernel(part_ref, out_ref):
    total = part_ref[0].astype(F32)
    for i in range(1, 8):
        total = total + part_ref[i].astype(F32)
    squares = total[:, 2 * SIZE : 2 * SIZE + 1] + total[:, 2 * SIZE + 1 : 2 * SIZE + 2]
    factor = lax.rsqrt(squares / D + norm_eps)
    gate = total[:, :SIZE] * factor
    up = total[:, SIZE : 2 * SIZE] * factor
    units = (gate * jax.nn.sigmoid(gate) * up).astype(BF)
    for i in range(16):
        out_ref[i] = units


def down_kernel(
    xl_ref, y_ref, own_ref, other_ref, w0, w1, hidden_ref, across_ref, place_ref, out_ref, total
):
    units = [
        jnp.concatenate(
            [own_ref[:, i].reshape(128, SIZE), other_ref[:, i].reshape(128, SIZE)], axis=0
        )
        for i in range(2)
    ]
    place = place_ref[...]
    none = jnp.zeros((128 - WIDTH, SIZE), BF)
    nt = (((1,), (1,)), ((), ()))
    for r, w in enumerate((w0, w1)):
        part = jnp.zeros((256, 128), F32)
        for i in range(2):
            at = i * DOWN
            wide = jnp.concatenate([w[:, at : at + SIZE], none], axis=0)
            part = part + lax.dot_general(units[i], wide, nt, preferred_element_type=F32)
        if r == 0:
            total[...] = part
            at = pl.multiple_of(y_ref[0] * 16, 16)
            total[pl.ds(at, 16), :] += hidden_ref[0:16, :]
            total[pl.ds(128 + at, 16), :] += across_ref[...]
            part = total[...]
        rows = dot(place, part.astype(BF)).astype(BF)
        out_ref[pl.ds((xl_ref[0] ^ r) * 8, 8)] = rows.reshape(8, 32, 128)


def swap(value, axis="c"):
    return lax.ppermute(value, axis, [(0, 1), (1, 0)])


def exchange(blocks, axes):
    return lax.all_to_all(blocks, axes, 0, 0, tiled=True)


def local(
    queries,
    new_latents,
    latent_cache,
    lengths,
    slot_of,
    value_maps,
    out_proj,
    residual,
    norm_gain,
    w_gate,
    w_up,
    w_down,
):
    xh, xl, core, tp = (lax.axis_index(a)[None].astype(jnp.int32) for a in ("xh", "xl", "c", "y"))

    blocks = call(
        attention_kernel,
        [SMEM, HBM, VMEM, HBM, HBM],
        shape((32, 16, 512)),
        [
            pltpu.VMEM((64, 576), BF),
            pltpu.VMEM((576, 512), BF),
            pltpu.VMEM((16, 512, 128), BF),
            pltpu.VMEM((4, 64, 128), F32),
            pltpu.VMEM((16, 512), F32),
            pltpu.SemaphoreType.DMA((3,)),
        ],
        200_000_000,
        4_000_000,
        56,
    )(lengths, queries.reshape(64, -1), new_latents[0], latent_cache[0].T, value_maps)
    blocks, out_proj, slot_of, residual, norm_gain, w_gate, w_up, w_down = lax.optimization_barrier(
        (blocks, out_proj.T, slot_of, residual.T, norm_gain, w_gate, w_up, w_down.T)
    )
    rows = exchange(blocks, ("z", "xh", "xl"))
    gains = jnp.broadcast_to(norm_gain[:, None], (WIDTH, 128))
    carry = jnp.concatenate([out_proj, residual, gains], axis=1)
    carry_other = swap(carry)
    tail, tail_other = carry[:, 2048:], carry_other[:, 2048:]

    *ff, down_own, down_sent = call(
        pack_kernel,
        [SMEM, SMEM, VMEM, VMEM, VMEM],
        [shape((WIDTH, 2 * SIZE))] * 4 + [shape((WIDTH, 2 * DOWN))] * 2,
        (),
        0,
        3_200_000,
    )(xh, xl, w_gate, w_up, w_down)
    ff = [
        ff[0],
        swap(ff[1], "xl"),
        swap(ff[2], "xh"),
        lax.ppermute(ff[3], ("xh", "xl"), [(i, 3 - i) for i in range(4)]),
    ]
    rows, ff[0] = lax.optimization_barrier((rows, ff[0]))
    part = call(
        out_kernel,
        [VMEM] * 3,
        shape((8, 32, 128)),
        [pltpu.VMEM((4, 512, 128), F32)],
        1_000_000,
        100_000,
    )(rows, out_proj, carry_other)
    pick, place = call(
        rows_kernel, [SMEM, SMEM, VMEM], [shape((16, 256)), shape((256, 256))], (), 0, 200_000
    )(core, tp, slot_of[None])
    part, *ff = lax.optimization_barrier((exchange(part, "y"), *ff))
    scaled, hidden = call(
        norm_kernel, [VMEM] * 4, [shape((32, 32, 128)), shape((32, 128), F32)], (), 0, 400_000
    )(part, pick, tail, tail_other)
    hidden, *ff = lax.optimization_barrier((hidden, *ff))
    ff_other = [swap(w) for w in ff]
    part = call(
        gate_kernel, [SMEM] * 2 + [VMEM] * 9, shape((8, 16, 1280)), (), 300_000_000, 2_800_000
    )(xh, xl, exchange(scaled, ("xh", "xl", "y")), *ff, *ff_other)
    _, hidden, down_sent = lax.optimization_barrier((part, hidden, down_sent))
    part, across, down_near = lax.optimization_barrier(
        (exchange(part, "z"), swap(hidden[16:]), swap(down_sent, "xl"))
    )
    units = call(units_kernel, [VMEM], shape((16, 16, SIZE)), (), 0, 500_000)(part)
    units = exchange(units, ("z", "xh"))
    part = call(
        down_kernel,
        [SMEM] * 2 + [VMEM] * 7,
        shape((16, 32, 128)),
        [pltpu.VMEM((256, 128), F32)],
        200_000_000,
        1_600_000,
    )(
        xl,
        tp,
        units.reshape(8, 2, 16, SIZE),
        swap(units).reshape(8, 2, 16, SIZE),
        down_own,
        down_near,
        hidden,
        across,
        place,
    )
    return jnp.sum(exchange(part, ("xl", "y"))[:, :, :WIDTH].astype(F32), axis=0).astype(BF)


def solution(mesh):
    fine = Mesh(mesh.devices.reshape(8, 2, 2, 2, 8), AXES)
    specs = (
        P(DP, None, "y", None),
        P(DP, None, None),
        P(DP, None, None),
        P(DP),
        P(),
        P("y", None, None),
        P("y", DP),
        P(None, DP),
        P(DP),
        P(DP, "y"),
        P(DP, "y"),
        P("y", DP),
    )
    return jax.shard_map(
        local, mesh=fine, in_specs=specs, out_specs=P("y", DP), check_vma=False
    )
```

```python
import jax
import jax.numpy as jnp
from jax import lax
from jax.experimental import pallas as pl
from jax.experimental.pallas import tpu as pltpu
from jax.sharding import Mesh
from jax.sharding import PartitionSpec as P

D = 7168
WIDTH = 112
SIZE = 576

score_scale = 192.0 ** (-0.5)
norm_eps = 1e-06

AXES = ("z", "xh", "xl", "c", "y")
DP = ("z", "xh", "xl", "c")
BF = jnp.bfloat16
F32 = jnp.float32
VMEM = pl.BlockSpec(memory_space=pltpu.VMEM)
SMEM = pl.BlockSpec(memory_space=pltpu.SMEM)
HBM = pl.BlockSpec(memory_space=pltpu.HBM)


def call(kernel, in_specs, outs, scratch=(), flops=0, moved=0, limit=24):
    many = isinstance(outs, (list, tuple))
    return pl.pallas_call(
        kernel,
        in_specs=in_specs,
        out_specs=[VMEM] * len(outs) if many else VMEM,
        out_shape=list(outs) if many else outs,
        scratch_shapes=list(scratch),
        compiler_params=pltpu.CompilerParams(vmem_limit_bytes=limit * 1024 * 1024),
        cost_estimate=pl.CostEstimate(flops=flops, bytes_accessed=moved, transcendentals=0),
    )


def shape(dims, dtype=BF):
    return jax.ShapeDtypeStruct(dims, dtype)


def dot(a, b):
    return jnp.dot(a, b, preferred_element_type=F32)


def attention_kernel(len_ref, q_ref, new_ref, cache_ref, maps_ref, out_ref, q_in, cache, maps, ctx, pairs, heads, sems):
    fetches = [
        pltpu.make_async_copy(src, dst, sems.at[i])
        for i, (src, dst) in enumerate(((q_ref, q_in), (cache_ref, cache), (maps_ref, maps)))
    ]
    for fetch in fetches:
        fetch.start()
    new = new_ref[...]
    nt = (((1,), (1,)), ((), ()))
    fetches[0].wait()
    q = q_in[...]
    fresh = lax.dot_general(q, new, nt, preferred_element_type=F32) * score_scale
    fetches[1].wait()
    score = dot(q, cache[...]) * score_scale
    keep = lax.broadcasted_iota(jnp.int32, score.shape, 1) < len_ref[0]
    step = lax.broadcasted_iota(jnp.int32, fresh.shape, 0) // 16
    keep_new = lax.broadcasted_iota(jnp.int32, fresh.shape, 1) <= step
    score = jnp.where(keep, score, -1e30)
    fresh = jnp.where(keep_new, fresh, -1e30)
    top = jnp.maximum(
        jnp.max(score, axis=1, keepdims=True), jnp.max(fresh, axis=1, keepdims=True)
    )
    weight = jnp.where(keep, jnp.exp(score - top), 0.0)
    weight_new = jnp.where(keep_new, jnp.exp(fresh - top), 0.0)
    total = jnp.sum(weight, axis=1, keepdims=True) + jnp.sum(weight_new, axis=1, keepdims=True)
    prob = (weight / total).astype(BF)
    prob_new = (weight_new / total).astype(BF)
    context = lax.dot_general(prob, cache[:512, :], nt, preferred_element_type=F32)
    context = (context + dot(prob_new, new[:, :512])).astype(BF).astype(F32)
    for n in range(4):
        ctx[n] = context[:, n * 128 : (n + 1) * 128]
    fetches[2].wait()
    for h in range(8):
        rows = jnp.concatenate([ctx[n, pl.ds(h, 8, stride=8), :] for n in range(4)], axis=1).astype(BF)
        pair = dot(rows, jnp.concatenate([maps[h], maps[h + 8]], axis=1))
        for i, head in enumerate((h, h + 8)):
            pairs[i] = pair[:, i * 128 : i * 128 + 128]
            k, place = head // 4, head % 4
            heads[k * 4 : k * 4 + 4, place * 128 : place * 128 + 128] = pairs[i, pl.ds(i, 4, stride=2), :]
    block = heads[...].astype(BF)
    for i in range(32):
        out_ref[i] = block


def target(xh_ref, xl_ref, r):
    return 2 * (xh_ref[0] ^ (r >> 1)) + (xl_ref[0] ^ (r & 1))


def pack_kernel(xh_ref, xl_ref, gate_ref, up_ref, proj_ref, residual_ref, gain_ref, carry_ref, *outs):
    carry_ref[:, :2048] = proj_ref[...]
    carry_ref[:, 2048:2304] = residual_ref[...]
    carry_ref[:, 2304:] = gain_ref[...]
    for i in range(4):
        cut = slice(i * SIZE, (i + 1) * SIZE)
        block = jnp.concatenate([gate_ref[:, cut], up_ref[:, cut]], axis=1)
        for r, out_ref in enumerate(outs):

            @pl.when(target(xh_ref, xl_ref, r) == i)
            def _(out_ref=out_ref, block=block):
                out_ref[...] = block


def pack_down_kernel(xh_ref, xl_ref, down_ref, *outs):
    for i in range(4):
        block = down_ref[:, i * SIZE : (i + 1) * SIZE]
        for r, out_ref in enumerate(outs):

            @pl.when(target(xh_ref, xl_ref, r) == i)
            def _(out_ref=out_ref, block=block):
                out_ref[...] = block


def rows_kernel(core_ref, y_ref, slot_ref, pick_ref, place_ref):
    iota = lambda dims, axis: lax.broadcasted_iota(jnp.int32, dims, axis)
    slot = slot_ref[...].astype(F32)
    col = iota((256, 256), 1)
    core = jnp.where(col < 128, core_ref[0], 1 - core_ref[0])
    held = (col & 31) * 8 + core * 4 + ((col >> 5) & 3)
    spread = (iota((256, 64), 0) >> 2) == iota((256, 64), 1)
    of_row = jnp.sum(jnp.where(spread, slot, 0.0), axis=1, keepdims=True).astype(jnp.int32)
    place = (of_row * 4 + (iota((256, 256), 0) & 3)) == held
    place_ref[...] = jnp.where(place, 1.0, 0.0).astype(BF)
    across = jnp.where((iota((64, 256), 1) >> 2) == iota((64, 256), 0), 1.0, 0.0).astype(BF)
    of_col = dot(jnp.broadcast_to(slot, (16, 64)).astype(BF), across).astype(jnp.int32)
    own = iota((16, 256), 0) + y_ref[0] * 16
    held = (own & 31) * 8 + core_ref[0] * 4 + (own >> 5)
    pick_ref[...] = jnp.where(of_col * 4 + (iota((16, 256), 1) & 3) == held, 1.0, 0.0).astype(BF)


def out_kernel(x_ref, own_ref, other_ref, out_ref, wide):
    for n in range(4):
        wide[n] = x_ref[:, :, n * 128 : (n + 1) * 128].reshape(512, 128).astype(F32)
    pad = jnp.zeros((128 - WIDTH, 512), BF)
    total = jnp.zeros((128, 256), F32)
    for k in range(4):
        rows = []
        for t in range(4):
            tiles = [wide[n, pl.ds(k * 4 + t, 32, stride=16), :] for n in range(4)]
            rows.append(jnp.concatenate(tiles, axis=1).astype(BF))
        cut = slice(k * 512, (k + 1) * 512)
        w = jnp.concatenate([own_ref[:, cut], pad, other_ref[:, cut], pad], axis=0)
        total = total + lax.dot_general(
            jnp.concatenate(rows, axis=0), w, (((1,), (1,)), ((), ())), preferred_element_type=F32
        )
    total = total.astype(BF)
    for y in range(8):
        part = total[y * 16 : y * 16 + 16]
        out_ref[y, 0:16, :] = part[:, :128]
        out_ref[y, 16:32, :] = part[:, 128:]


def norm_kernel(part_ref, pick_ref, own_ref, other_ref, out_ref, hidden_ref):
    attended = part_ref[0].astype(F32)
    for i in range(1, 8):
        attended = attended + part_ref[i].astype(F32)
    attended = attended[:, :WIDTH]
    nt = (((1,), (1,)), ((), ()))
    pick = pick_ref[...]
    unit = (lax.broadcasted_iota(jnp.int32, (16, 128), 1) == 0).astype(F32).astype(BF)
    picked = lambda ref: lax.dot_general(pick, ref[:, 2048:2304], nt, preferred_element_type=F32)
    gains = lambda ref: lax.dot_general(unit, ref[:, 2304:], nt, preferred_element_type=F32)
    hidden = attended + jnp.concatenate([picked(own_ref), picked(other_ref)], axis=0)
    gain = jnp.concatenate([gains(own_ref), gains(other_ref)], axis=0)
    squares = jnp.sum(hidden * hidden, axis=1, keepdims=True)
    squares = squares[0:16] + squares[16:32]
    none = jnp.zeros((32, 128 - WIDTH), F32)
    scaled = jnp.concatenate([hidden * gain, none], axis=1)
    lane = lax.broadcasted_iota(jnp.int32, (32, 128), 1)
    first = lax.broadcasted_iota(jnp.int32, (32, 128), 0) < 16
    high = squares.astype(BF).astype(F32)
    twice = lambda a: jnp.concatenate([a, a], axis=0)
    scaled = jnp.where(first & (lane == WIDTH), twice(high), scaled)
    scaled = jnp.where(first & (lane == WIDTH + 1), twice(squares - high), scaled).astype(BF)
    hidden_ref[...] = jnp.concatenate([hidden, none], axis=1)
    for i in range(32):
        out_ref[i] = scaled


def gate_kernel(xh_ref, xl_ref, full_ref, *refs):
    own_refs, other_refs, out_ref = refs[:4], refs[4:7], refs[7]
    lane = lax.broadcasted_iota(jnp.int32, (128, 128), 1)
    valid = lane < WIDTH
    none = jnp.zeros((128 - WIDTH, 384), BF)
    zero = jnp.zeros((128, 128), BF)
    held, squares = [], jnp.zeros((128, 1), F32)
    for r in range(4):
        x = 2 * (xh_ref[0] ^ (r >> 1)) + (xl_ref[0] ^ (r & 1))
        block = full_ref[pl.ds(x * 8, 8)]
        own = block[:, 0:16, :].reshape(128, 128)
        other = block[:, 16:32, :].reshape(128, 128)
        sums = jnp.where((lane == WIDTH) | (lane == WIDTH + 1), own.astype(F32), 0.0)
        squares = squares + jnp.sum(sums, axis=1, keepdims=True)
        both = [jnp.where(valid, own, zero), jnp.where(valid, other, zero)]
        held.append(jnp.concatenate(both, axis=1))
    for n in range(0, 2 * SIZE, 384):
        total = jnp.zeros((128, 384), F32)
        for r in range(4):
            k, at = divmod(r * 2 * SIZE + n, 4 * 384)
            both = [own_refs[r][:, n : n + 384], none, other_refs[k][:, at : at + 384], none]
            total = total + dot(held[r], jnp.concatenate(both, axis=0))
        out_ref[:, :, n : n + 384] = total.astype(BF).reshape(8, 16, 384)
    high = squares.astype(BF).astype(F32)
    last = jnp.where(lane == 0, high, jnp.where(lane == 1, squares - high, 0.0))
    out_ref[:, :, 1152:1280] = last.astype(BF).reshape(8, 16, 128)


def units_kernel(part_ref, out_ref):
    total = part_ref[0].astype(F32)
    for i in range(1, 8):
        total = total + part_ref[i].astype(F32)
    squares = total[:, 2 * SIZE : 2 * SIZE + 1] + total[:, 2 * SIZE + 1 : 2 * SIZE + 2]
    factor = lax.rsqrt(squares / D + norm_eps)
    gate = total[:, :SIZE] * factor
    up = total[:, SIZE : 2 * SIZE] * factor
    units = (gate * jax.nn.sigmoid(gate) * up).astype(BF)
    for i in range(8):
        out_ref[i] = units


def down_kernel(
    xh_ref, xl_ref, y_ref, own_ref, other_ref, w0, w1, w2, w3, hidden_ref, across_ref, place_ref, out_ref, total
):
    units = jnp.concatenate([own_ref[...].reshape(128, SIZE), other_ref[...].reshape(128, SIZE)], axis=0)
    place = place_ref[...]
    none = jnp.zeros((128 - WIDTH, SIZE), BF)
    nt = (((1,), (1,)), ((), ()))
    for r, w in enumerate((w0, w1, w2, w3)):
        wide = jnp.concatenate([w[...], none], axis=0)
        part = lax.dot_general(units, wide, nt, preferred_element_type=F32)
        if r == 0:
            total[...] = part
            at = pl.multiple_of(y_ref[0] * 16, 16)
            total[pl.ds(at, 16), :] += hidden_ref[0:16, :]
            total[pl.ds(128 + at, 16), :] += across_ref[...]
            part = total[...]
        rows = dot(place, part.astype(BF)).astype(BF)
        x = 2 * (xh_ref[0] ^ (r >> 1)) + (xl_ref[0] ^ (r & 1))
        out_ref[pl.ds(x * 8, 8)] = rows.reshape(8, 32, 128)


def swap(value, axis="c"):
    return lax.ppermute(value, axis, [(0, 1), (1, 0)])


def exchange(blocks, axes):
    return lax.all_to_all(blocks, axes, 0, 0, tiled=True)


def diagonal(value):
    return lax.ppermute(value, ("xh", "xl"), [(i, 3 - i) for i in range(4)])


def local(
    queries,
    new_latents,
    latent_cache,
    lengths,
    slot_of,
    value_maps,
    out_proj,
    residual,
    norm_gain,
    w_gate,
    w_up,
    w_down,
):
    xh, xl, core, tp = (lax.axis_index(a)[None].astype(jnp.int32) for a in ("xh", "xl", "c", "y"))

    blocks = call(
        attention_kernel,
        [SMEM, HBM, VMEM, HBM, HBM],
        shape((32, 16, 512)),
        [
            pltpu.VMEM((64, 576), BF),
            pltpu.VMEM((576, 512), BF),
            pltpu.VMEM((16, 512, 128), BF),
            pltpu.VMEM((4, 64, 128), F32),
            pltpu.VMEM((2, 8, 128), F32),
            pltpu.VMEM((16, 512), F32),
            pltpu.SemaphoreType.DMA((3,)),
        ],
        200_000_000,
        4_000_000,
        56,
    )(lengths, queries.reshape(64, -1), new_latents[0], latent_cache[0].T, value_maps)
    blocks, out_proj, slot_of, residual, norm_gain, w_gate, w_up, w_down = lax.optimization_barrier(
        (blocks, out_proj.T, slot_of, residual.T, norm_gain, w_gate, w_up, w_down.T)
    )
    rows = exchange(blocks, ("z", "xh", "xl"))
    gains = jnp.broadcast_to(norm_gain[:, None], (WIDTH, 128))
    carry, *ff = call(
        pack_kernel,
        [SMEM] * 2 + [VMEM] * 5,
        [shape((WIDTH, 2048 + 256 + 128))] + [shape((WIDTH, 2 * SIZE))] * 4,
        (),
        0,
        3_200_000,
    )(xh, xl, w_gate, w_up, out_proj, residual, gains)
    carry_other = swap(carry)
    ff = [ff[0], swap(ff[1], "xl"), swap(ff[2], "xh"), diagonal(ff[3])]
    rows, ff[0] = lax.optimization_barrier((rows, ff[0]))
    part = call(
        out_kernel,
        [VMEM] * 3,
        shape((8, 32, 128)),
        [pltpu.VMEM((4, 512, 128), F32)],
        1_000_000,
        100_000,
    )(rows, out_proj, carry_other)
    _, slot_of, w_down = lax.optimization_barrier((part, slot_of, w_down))
    pick, place = call(
        rows_kernel, [SMEM, SMEM, VMEM], [shape((16, 256)), shape((256, 256))], (), 0, 200_000
    )(core, tp, slot_of[None])
    down = call(
        pack_down_kernel, [SMEM, SMEM, VMEM], [shape((WIDTH, SIZE))] * 4, (), 0, 1_000_000
    )(xh, xl, w_down)
    _, _, ff = lax.optimization_barrier((pick, down, ff))
    joined = jnp.concatenate
    thirds = [
        joined([ff[0], ff[1][:, :384]], axis=1),
        joined([ff[1][:, 384:], ff[2][:, :768]], axis=1),
        joined([ff[2][:, 768:], ff[3]], axis=1),
    ]
    part, ff, thirds, down, pick = lax.optimization_barrier(
        (exchange(part, "y"), ff, thirds, down, pick)
    )
    scaled, hidden = call(
        norm_kernel, [VMEM] * 4, [shape((32, 32, 128)), shape((32, 128), F32)], (), 0, 400_000
    )(part, pick, carry, carry_other)
    hidden, *thirds = lax.optimization_barrier((hidden, *thirds))
    ff_other = [swap(w) for w in thirds]
    part = call(
        gate_kernel, [SMEM] * 2 + [VMEM] * 8, shape((8, 16, 1280)), (), 300_000_000, 2_800_000
    )(xh, xl, exchange(scaled, ("xh", "xl", "y")), *ff, *ff_other)
    _, far, near = lax.optimization_barrier((part, down[2], down[1]))
    part, far, near = lax.optimization_barrier(
        (exchange(part, "z"), swap(far, "xh"), swap(near, "xl"))
    )
    units = call(units_kernel, [VMEM], shape((8, 16, SIZE)), (), 0, 500_000)(part)
    _, hidden, cross = lax.optimization_barrier((units, hidden, down[3]))
    units, across, cross = lax.optimization_barrier(
        (exchange(units, "z"), swap(hidden[16:]), diagonal(cross))
    )
    down = (down[0], near, far, cross)
    part = call(
        down_kernel,
        [SMEM] * 3 + [VMEM] * 9,
        shape((32, 32, 128)),
        [pltpu.VMEM((256, 128), F32)],
        200_000_000,
        1_600_000,
    )(xh, xl, tp, units, swap(units), *down, hidden, across, place)
    total = jnp.sum(exchange(part, ("xh", "xl", "y"))[:, :, :WIDTH].astype(F32), axis=0)
    return total.astype(BF)


def solution(mesh):
    fine = Mesh(mesh.devices.reshape(8, 2, 2, 2, 8), AXES)
    specs = (
        P(DP, None, "y", None),
        P(DP, None, None),
        P(DP, None, None),
        P(DP),
        P(),
        P("y", None, None),
        P("y", DP),
        P(None, DP),
        P(DP),
        P(DP, "y"),
        P(DP, "y"),
        P("y", DP),
    )
    return jax.shard_map(
        local, mesh=fine, in_specs=specs, out_specs=P("y", DP), check_vma=False
    )
```

```python
import jax
import jax.numpy as jnp
from jax import lax
from jax.experimental import pallas as pl
from jax.experimental.pallas import tpu as pltpu
from jax.sharding import Mesh
from jax.sharding import PartitionSpec as P

D = 7168
WIDTH = 112
SIZE = 576

score_scale = 192.0 ** (-0.5)
norm_eps = 1e-06

AXES = ("z", "xh", "xl", "c", "y")
DP = ("z", "xh", "xl", "c")
BF = jnp.bfloat16
F32 = jnp.float32
VMEM = pl.BlockSpec(memory_space=pltpu.VMEM)
SMEM = pl.BlockSpec(memory_space=pltpu.SMEM)
HBM = pl.BlockSpec(memory_space=pltpu.HBM)


def call(kernel, in_specs, outs, scratch=(), flops=0, moved=0, limit=24):
    many = isinstance(outs, (list, tuple))
    return pl.pallas_call(
        kernel,
        in_specs=in_specs,
        out_specs=[VMEM] * len(outs) if many else VMEM,
        out_shape=list(outs) if many else outs,
        scratch_shapes=list(scratch),
        compiler_params=pltpu.CompilerParams(vmem_limit_bytes=limit * 1024 * 1024),
        cost_estimate=pl.CostEstimate(flops=flops, bytes_accessed=moved, transcendentals=0),
    )


def shape(dims, dtype=BF):
    return jax.ShapeDtypeStruct(dims, dtype)


def dot(a, b):
    return jnp.dot(a, b, preferred_element_type=F32)


def attention_kernel(len_ref, q_ref, new_ref, cache_ref, maps_ref, out_ref, q_in, cache, maps, ctx, pairs, heads, sems):
    fetches = [
        pltpu.make_async_copy(src, dst, sems.at[i])
        for i, (src, dst) in enumerate(((q_ref, q_in), (cache_ref, cache), (maps_ref, maps)))
    ]
    for fetch in fetches:
        fetch.start()
    new = new_ref[...]
    nt = (((1,), (1,)), ((), ()))
    fetches[0].wait()
    q = q_in[...]
    fresh = lax.dot_general(q, new, nt, preferred_element_type=F32) * score_scale
    fetches[1].wait()
    score = dot(q, cache[...]) * score_scale
    keep = lax.broadcasted_iota(jnp.int32, score.shape, 1) < len_ref[0]
    step = lax.broadcasted_iota(jnp.int32, fresh.shape, 0) // 16
    keep_new = lax.broadcasted_iota(jnp.int32, fresh.shape, 1) <= step
    score = jnp.where(keep, score, -1e30)
    fresh = jnp.where(keep_new, fresh, -1e30)
    top = jnp.maximum(
        jnp.max(score, axis=1, keepdims=True), jnp.max(fresh, axis=1, keepdims=True)
    )
    weight = jnp.where(keep, jnp.exp(score - top), 0.0)
    weight_new = jnp.where(keep_new, jnp.exp(fresh - top), 0.0)
    total = jnp.sum(weight, axis=1, keepdims=True) + jnp.sum(weight_new, axis=1, keepdims=True)
    prob = (weight / total).astype(BF)
    prob_new = (weight_new / total).astype(BF)
    context = lax.dot_general(prob, cache[:512, :], nt, preferred_element_type=F32)
    context = (context + dot(prob_new, new[:, :512])).astype(BF).astype(F32)
    for n in range(4):
        ctx[n] = context[:, n * 128 : (n + 1) * 128]
    fetches[2].wait()
    for h in range(8):
        rows = jnp.concatenate([ctx[n, pl.ds(h, 8, stride=8), :] for n in range(4)], axis=1).astype(BF)
        pair = dot(rows, jnp.concatenate([maps[h], maps[h + 8]], axis=1))
        for i, head in enumerate((h, h + 8)):
            pairs[i] = pair[:, i * 128 : i * 128 + 128]
            k, place = head // 4, head % 4
            heads[k * 4 : k * 4 + 4, place * 128 : place * 128 + 128] = pairs[i, pl.ds(i, 4, stride=2), :]
    block = heads[...].astype(BF)
    for i in range(32):
        out_ref[i] = block


def target(xh_ref, xl_ref, r):
    return 2 * (xh_ref[0] ^ (r >> 1)) + (xl_ref[0] ^ (r & 1))


def pack_kernel(xh_ref, xl_ref, gate_ref, up_ref, down_ref, proj_ref, residual_ref, gain_ref, carry_ref, *outs):
    carry_ref[:, :2048] = proj_ref[...]
    carry_ref[:, 2048:2304] = residual_ref[...]
    carry_ref[:, 2304:] = gain_ref[...]
    for i in range(4):
        cut = slice(i * SIZE, (i + 1) * SIZE)
        block = jnp.concatenate([gate_ref[:, cut], up_ref[:, cut]], axis=1)
        for r, out_ref in enumerate(outs):

            @pl.when(target(xh_ref, xl_ref, r) == i)
            def _(out_ref=out_ref, block=block, down=down_ref[:, cut] if r == 1 else None):
                out_ref[:, : 2 * SIZE] = block
                if down is not None:
                    out_ref[:, 2 * SIZE :] = down


def pack_down_kernel(xh_ref, xl_ref, down_ref, *outs):
    for i in range(4):
        block = down_ref[:, i * SIZE : (i + 1) * SIZE]
        for r, out_ref in zip((0, 2, 3), outs):

            @pl.when(target(xh_ref, xl_ref, r) == i)
            def _(out_ref=out_ref, block=block):
                out_ref[...] = block


def rows_kernel(core_ref, y_ref, slot_ref, pick_ref, place_ref):
    iota = lambda dims, axis: lax.broadcasted_iota(jnp.int32, dims, axis)
    slot = slot_ref[...].astype(F32)
    col = iota((256, 256), 1)
    core = jnp.where(col < 128, core_ref[0], 1 - core_ref[0])
    held = (col & 31) * 8 + core * 4 + ((col >> 5) & 3)
    spread = (iota((256, 64), 0) >> 2) == iota((256, 64), 1)
    of_row = jnp.sum(jnp.where(spread, slot, 0.0), axis=1, keepdims=True).astype(jnp.int32)
    place = (of_row * 4 + (iota((256, 256), 0) & 3)) == held
    place_ref[...] = jnp.where(place, 1.0, 0.0).astype(BF)
    across = jnp.where((iota((64, 256), 1) >> 2) == iota((64, 256), 0), 1.0, 0.0).astype(BF)
    of_col = dot(jnp.broadcast_to(slot, (16, 64)).astype(BF), across).astype(jnp.int32)
    own = iota((16, 256), 0) + y_ref[0] * 16
    held = (own & 31) * 8 + core_ref[0] * 4 + (own >> 5)
    pick_ref[...] = jnp.where(of_col * 4 + (iota((16, 256), 1) & 3) == held, 1.0, 0.0).astype(BF)


def out_kernel(x_ref, own_ref, other_ref, out_ref, wide):
    for n in range(4):
        wide[n] = x_ref[:, :, n * 128 : (n + 1) * 128].reshape(512, 128).astype(F32)
    pad = jnp.zeros((128 - WIDTH, 512), BF)
    total = jnp.zeros((128, 256), F32)
    for k in range(4):
        rows = []
        for t in range(4):
            tiles = [wide[n, pl.ds(k * 4 + t, 32, stride=16), :] for n in range(4)]
            rows.append(jnp.concatenate(tiles, axis=1).astype(BF))
        cut = slice(k * 512, (k + 1) * 512)
        w = jnp.concatenate([own_ref[:, cut], pad, other_ref[:, cut], pad], axis=0)
        total = total + lax.dot_general(
            jnp.concatenate(rows, axis=0), w, (((1,), (1,)), ((), ())), preferred_element_type=F32
        )
    total = total.astype(BF)
    for y in range(8):
        part = total[y * 16 : y * 16 + 16]
        out_ref[y, 0:16, :] = part[:, :128]
        out_ref[y, 16:32, :] = part[:, 128:]


def norm_kernel(part_ref, pick_ref, own_ref, other_ref, out_ref, hidden_ref):
    attended = part_ref[0].astype(F32)
    for i in range(1, 8):
        attended = attended + part_ref[i].astype(F32)
    attended = attended[:, :WIDTH]
    nt = (((1,), (1,)), ((), ()))
    pick = pick_ref[...]
    unit = (lax.broadcasted_iota(jnp.int32, (16, 128), 1) == 0).astype(F32).astype(BF)
    picked = lambda ref: lax.dot_general(pick, ref[:, 2048:2304], nt, preferred_element_type=F32)
    gains = lambda ref: lax.dot_general(unit, ref[:, 2304:], nt, preferred_element_type=F32)
    hidden = attended + jnp.concatenate([picked(own_ref), picked(other_ref)], axis=0)
    gain = jnp.concatenate([gains(own_ref), gains(other_ref)], axis=0)
    squares = jnp.sum(hidden * hidden, axis=1, keepdims=True)
    squares = squares[0:16] + squares[16:32]
    none = jnp.zeros((32, 128 - WIDTH), F32)
    scaled = jnp.concatenate([hidden * gain, none], axis=1)
    lane = lax.broadcasted_iota(jnp.int32, (32, 128), 1)
    first = lax.broadcasted_iota(jnp.int32, (32, 128), 0) < 16
    high = squares.astype(BF).astype(F32)
    twice = lambda a: jnp.concatenate([a, a], axis=0)
    scaled = jnp.where(first & (lane == WIDTH), twice(high), scaled)
    scaled = jnp.where(first & (lane == WIDTH + 1), twice(squares - high), scaled).astype(BF)
    hidden_ref[...] = jnp.concatenate([hidden, none], axis=1)
    for i in range(32):
        out_ref[i] = scaled


def gate_kernel(xh_ref, xl_ref, full_ref, *refs):
    own_refs, other_refs, out_ref = refs[:4], refs[4:7], refs[7]
    lane = lax.broadcasted_iota(jnp.int32, (128, 128), 1)
    valid = lane < WIDTH
    none = jnp.zeros((128 - WIDTH, 384), BF)
    zero = jnp.zeros((128, 128), BF)
    held, squares = [], jnp.zeros((128, 1), F32)
    for r in range(4):
        x = 2 * (xh_ref[0] ^ (r >> 1)) + (xl_ref[0] ^ (r & 1))
        block = full_ref[pl.ds(x * 8, 8)]
        own = block[:, 0:16, :].reshape(128, 128)
        other = block[:, 16:32, :].reshape(128, 128)
        sums = jnp.where((lane == WIDTH) | (lane == WIDTH + 1), own.astype(F32), 0.0)
        squares = squares + jnp.sum(sums, axis=1, keepdims=True)
        both = [jnp.where(valid, own, zero), jnp.where(valid, other, zero)]
        held.append(jnp.concatenate(both, axis=1))
    for n in range(0, 2 * SIZE, 384):
        total = jnp.zeros((128, 384), F32)
        for r in range(4):
            k, at = divmod(r * 2 * SIZE + n, 4 * 384)
            both = [own_refs[r][:, n : n + 384], none, other_refs[k][:, at : at + 384], none]
            total = total + dot(held[r], jnp.concatenate(both, axis=0))
        out_ref[:, :, n : n + 384] = total.astype(BF).reshape(8, 16, 384)
    high = squares.astype(BF).astype(F32)
    last = jnp.where(lane == 0, high, jnp.where(lane == 1, squares - high, 0.0))
    out_ref[:, :, 1152:1280] = last.astype(BF).reshape(8, 16, 128)


def units_kernel(part_ref, out_ref):
    total = part_ref[0].astype(F32)
    for i in range(1, 8):
        total = total + part_ref[i].astype(F32)
    squares = total[:, 2 * SIZE : 2 * SIZE + 1] + total[:, 2 * SIZE + 1 : 2 * SIZE + 2]
    factor = lax.rsqrt(squares / D + norm_eps)
    gate = total[:, :SIZE] * factor
    up = total[:, SIZE : 2 * SIZE] * factor
    units = (gate * jax.nn.sigmoid(gate) * up).astype(BF)
    for i in range(8):
        out_ref[i] = units


def down_kernel(
    xh_ref, xl_ref, y_ref, own_ref, other_ref, w0, w1, w2, w3, hidden_ref, across_ref, place_ref, out_ref, total
):
    units = jnp.concatenate([own_ref[...].reshape(128, SIZE), other_ref[...].reshape(128, SIZE)], axis=0)
    place = place_ref[...]
    none = jnp.zeros((128 - WIDTH, SIZE), BF)
    nt = (((1,), (1,)), ((), ()))
    for r, w in enumerate((w0, w1, w2, w3)):
        wide = jnp.concatenate([w[:, w.shape[1] - SIZE :], none], axis=0)
        part = lax.dot_general(units, wide, nt, preferred_element_type=F32)
        if r == 0:
            total[...] = part
            at = pl.multiple_of(y_ref[0] * 16, 16)
            total[pl.ds(at, 16), :] += hidden_ref[0:16, :]
            total[pl.ds(128 + at, 16), :] += across_ref[...]
            part = total[...]
        rows = dot(place, part.astype(BF)).astype(BF)
        x = 2 * (xh_ref[0] ^ (r >> 1)) + (xl_ref[0] ^ (r & 1))
        out_ref[pl.ds(x * 8, 8)] = rows.reshape(8, 32, 128)


def swap(value, axis="c"):
    return lax.ppermute(value, axis, [(0, 1), (1, 0)])


def exchange(blocks, axes):
    return lax.all_to_all(blocks, axes, 0, 0, tiled=True)


def diagonal(value):
    return lax.ppermute(value, ("xh", "xl"), [(i, 3 - i) for i in range(4)])


def local(
    queries,
    new_latents,
    latent_cache,
    lengths,
    slot_of,
    value_maps,
    out_proj,
    residual,
    norm_gain,
    w_gate,
    w_up,
    w_down,
):
    xh, xl, core, tp = (lax.axis_index(a)[None].astype(jnp.int32) for a in ("xh", "xl", "c", "y"))

    blocks = call(
        attention_kernel,
        [SMEM, HBM, VMEM, HBM, HBM],
        shape((32, 16, 512)),
        [
            pltpu.VMEM((64, 576), BF),
            pltpu.VMEM((576, 512), BF),
            pltpu.VMEM((16, 512, 128), BF),
            pltpu.VMEM((4, 64, 128), F32),
            pltpu.VMEM((2, 8, 128), F32),
            pltpu.VMEM((16, 512), F32),
            pltpu.SemaphoreType.DMA((3,)),
        ],
        200_000_000,
        4_000_000,
        56,
    )(lengths, queries.reshape(64, -1), new_latents[0], latent_cache[0].T, value_maps)
    blocks, out_proj, slot_of, residual, norm_gain, w_gate, w_up, w_down = lax.optimization_barrier(
        (blocks, out_proj.T, slot_of, residual.T, norm_gain, w_gate, w_up, w_down.T)
    )
    rows = exchange(blocks, ("z", "xh", "xl"))
    gains = jnp.broadcast_to(norm_gain[:, None], (WIDTH, 128))
    carry, *ff = call(
        pack_kernel,
        [SMEM] * 2 + [VMEM] * 6,
        [shape((WIDTH, 2048 + 256 + 128))]
        + [shape((WIDTH, n * SIZE)) for n in (2, 3, 2, 2)],
        (),
        0,
        3_200_000,
    )(xh, xl, w_gate, w_up, w_down, out_proj, residual, gains)
    carry_other = swap(carry)
    ff = [ff[0], swap(ff[1], "xl"), swap(ff[2], "xh"), diagonal(ff[3])]
    rows, ff[0] = lax.optimization_barrier((rows, ff[0]))
    part = call(
        out_kernel,
        [VMEM] * 3,
        shape((8, 32, 128)),
        [pltpu.VMEM((4, 512, 128), F32)],
        1_000_000,
        100_000,
    )(rows, out_proj, carry_other)
    _, slot_of, w_down = lax.optimization_barrier((part, slot_of, w_down))
    pick, place = call(
        rows_kernel, [SMEM, SMEM, VMEM], [shape((16, 256)), shape((256, 256))], (), 0, 200_000
    )(core, tp, slot_of[None])
    down = call(
        pack_down_kernel, [SMEM, SMEM, VMEM], [shape((WIDTH, SIZE))] * 3, (), 0, 1_000_000
    )(xh, xl, w_down)
    _, _, ff = lax.optimization_barrier((pick, down, ff))
    joined = jnp.concatenate
    thirds = [
        joined([ff[0], ff[1][:, :384]], axis=1),
        joined([ff[1][:, 384 : 2 * SIZE], ff[2][:, :768]], axis=1),
        joined([ff[2][:, 768:], ff[3]], axis=1),
    ]
    part, ff, thirds, down, pick = lax.optimization_barrier(
        (exchange(part, "y"), ff, thirds, down, pick)
    )
    scaled, hidden = call(
        norm_kernel, [VMEM] * 4, [shape((32, 32, 128)), shape((32, 128), F32)], (), 0, 400_000
    )(part, pick, carry, carry_other)
    hidden, *thirds = lax.optimization_barrier((hidden, *thirds))
    ff_other = [swap(w) for w in thirds]
    part = call(
        gate_kernel, [SMEM] * 2 + [VMEM] * 8, shape((8, 16, 1280)), (), 300_000_000, 2_800_000
    )(xh, xl, exchange(scaled, ("xh", "xl", "y")), *ff, *ff_other)
    _, hidden, far = lax.optimization_barrier((part, hidden, down[1]))
    part, far, across = lax.optimization_barrier(
        (exchange(part, "z"), swap(far, "xh"), swap(hidden[16:]))
    )
    units = call(units_kernel, [VMEM], shape((8, 16, SIZE)), (), 0, 500_000)(part)
    _, cross = lax.optimization_barrier((units, down[2]))
    units, cross = lax.optimization_barrier((exchange(units, "z"), diagonal(cross)))
    down = (down[0], ff[1], far, cross)
    part = call(
        down_kernel,
        [SMEM] * 3 + [VMEM] * 9,
        shape((32, 32, 128)),
        [pltpu.VMEM((256, 128), F32)],
        200_000_000,
        1_600_000,
    )(xh, xl, tp, units, swap(units), *down, hidden, across, place)
    total = jnp.sum(exchange(part, ("xh", "xl", "y"))[:, :, :WIDTH].astype(F32), axis=0)
    return total.astype(BF)


def solution(mesh):
    fine = Mesh(mesh.devices.reshape(8, 2, 2, 2, 8), AXES)
    specs = (
        P(DP, None, "y", None),
        P(DP, None, None),
        P(DP, None, None),
        P(DP),
        P(),
        P("y", None, None),
        P("y", DP),
        P(None, DP),
        P(DP),
        P(DP, "y"),
        P(DP, "y"),
        P("y", DP),
    )
    return jax.shard_map(
        local, mesh=fine, in_specs=specs, out_specs=P("y", DP), check_vma=False
    )
```

```python
import jax
import jax.numpy as jnp
from jax import lax
from jax.experimental import pallas as pl
from jax.experimental.pallas import tpu as pltpu
from jax.sharding import Mesh
from jax.sharding import PartitionSpec as P

D = 7168
WIDTH = 112
SIZE = 576

score_scale = 192.0 ** (-0.5)
norm_eps = 1e-06

AXES = ("z", "xh", "xl", "c", "y")
DP = ("z", "xh", "xl", "c")
BF = jnp.bfloat16
F32 = jnp.float32
VMEM = pl.BlockSpec(memory_space=pltpu.VMEM)
SMEM = pl.BlockSpec(memory_space=pltpu.SMEM)
HBM = pl.BlockSpec(memory_space=pltpu.HBM)


def call(kernel, in_specs, outs, scratch=(), flops=0, moved=0, limit=24):
    many = isinstance(outs, (list, tuple))
    return pl.pallas_call(
        kernel,
        in_specs=in_specs,
        out_specs=[VMEM] * len(outs) if many else VMEM,
        out_shape=list(outs) if many else outs,
        scratch_shapes=list(scratch),
        compiler_params=pltpu.CompilerParams(vmem_limit_bytes=limit * 1024 * 1024),
        cost_estimate=pl.CostEstimate(flops=flops, bytes_accessed=moved, transcendentals=0),
    )


def shape(dims, dtype=BF):
    return jax.ShapeDtypeStruct(dims, dtype)


def dot(a, b):
    return jnp.dot(a, b, preferred_element_type=F32)


def attention_kernel(len_ref, q_ref, new_ref, cache_ref, maps_ref, out_ref, q_in, cache, maps, ctx, pairs, heads, sems):
    fetches = [
        pltpu.make_async_copy(src, dst, sems.at[i])
        for i, (src, dst) in enumerate(((q_ref, q_in), (cache_ref, cache), (maps_ref, maps)))
    ]
    for fetch in fetches:
        fetch.start()
    new = new_ref[...]
    nt = (((1,), (1,)), ((), ()))
    fetches[0].wait()
    q = q_in[...]
    fresh = lax.dot_general(q, new, nt, preferred_element_type=F32) * score_scale
    fetches[1].wait()
    score = dot(q, cache[...]) * score_scale
    keep = lax.broadcasted_iota(jnp.int32, score.shape, 1) < len_ref[0]
    step = lax.broadcasted_iota(jnp.int32, fresh.shape, 0) // 16
    keep_new = lax.broadcasted_iota(jnp.int32, fresh.shape, 1) <= step
    score = jnp.where(keep, score, -1e30)
    fresh = jnp.where(keep_new, fresh, -1e30)
    top = jnp.maximum(
        jnp.max(score, axis=1, keepdims=True), jnp.max(fresh, axis=1, keepdims=True)
    )
    weight = jnp.where(keep, jnp.exp(score - top), 0.0)
    weight_new = jnp.where(keep_new, jnp.exp(fresh - top), 0.0)
    total = jnp.sum(weight, axis=1, keepdims=True) + jnp.sum(weight_new, axis=1, keepdims=True)
    prob = (weight / total).astype(BF)
    prob_new = (weight_new / total).astype(BF)
    context = lax.dot_general(prob, cache[:512, :], nt, preferred_element_type=F32)
    context = (context + dot(prob_new, new[:, :512])).astype(BF).astype(F32)
    for n in range(4):
        ctx[n] = context[:, n * 128 : (n + 1) * 128]
    fetches[2].wait()
    for h in range(8):
        rows = jnp.concatenate([ctx[n, pl.ds(h, 8, stride=8), :] for n in range(4)], axis=1).astype(BF)
        pair = dot(rows, jnp.concatenate([maps[h], maps[h + 8]], axis=1))
        for i, head in enumerate((h, h + 8)):
            pairs[i] = pair[:, i * 128 : i * 128 + 128]
            k, place = head // 4, head % 4
            heads[k * 4 : k * 4 + 4, place * 128 : place * 128 + 128] = pairs[i, pl.ds(i, 4, stride=2), :]
    block = heads[...].astype(BF)
    for i in range(32):
        out_ref[i] = block


def target(xh_ref, xl_ref, r):
    return 2 * (xh_ref[0] ^ (r >> 1)) + (xl_ref[0] ^ (r & 1))


def pack_kernel(xh_ref, xl_ref, gate_ref, up_ref, down_ref, proj_ref, residual_ref, gain_ref, carry_ref, *outs):
    carry_ref[:, :2048] = proj_ref[...]
    carry_ref[:, 2048:2304] = residual_ref[...]
    carry_ref[:, 2304:] = gain_ref[...]
    for i in range(4):
        cut = slice(i * SIZE, (i + 1) * SIZE)
        block = jnp.concatenate([gate_ref[:, cut], up_ref[:, cut]], axis=1)
        for r, out_ref in enumerate(outs):

            @pl.when(target(xh_ref, xl_ref, r) == i)
            def _(out_ref=out_ref, block=block, down=down_ref[:, cut] if r == 1 else None):
                out_ref[:, : 2 * SIZE] = block
                if down is not None:
                    out_ref[:, 2 * SIZE :] = down


def pack_down_kernel(xh_ref, xl_ref, down_ref, *outs):
    for i in range(4):
        block = down_ref[:, i * SIZE : (i + 1) * SIZE]
        for r, out_ref in zip((0, 2, 3), outs):

            @pl.when(target(xh_ref, xl_ref, r) == i)
            def _(out_ref=out_ref, block=block):
                out_ref[...] = block


def rows_kernel(core_ref, y_ref, slot_ref, pick_ref, place_ref):
    iota = lambda dims, axis: lax.broadcasted_iota(jnp.int32, dims, axis)
    slot = slot_ref[...].astype(F32)
    col = iota((256, 256), 1)
    core = jnp.where(col < 128, core_ref[0], 1 - core_ref[0])
    held = (col & 31) * 8 + core * 4 + ((col >> 5) & 3)
    spread = (iota((256, 64), 0) >> 2) == iota((256, 64), 1)
    of_row = jnp.sum(jnp.where(spread, slot, 0.0), axis=1, keepdims=True).astype(jnp.int32)
    place = (of_row * 4 + (iota((256, 256), 0) & 3)) == held
    place_ref[...] = jnp.where(place, 1.0, 0.0).astype(BF)
    across = jnp.where((iota((64, 256), 1) >> 2) == iota((64, 256), 0), 1.0, 0.0).astype(BF)
    of_col = dot(jnp.broadcast_to(slot, (16, 64)).astype(BF), across).astype(jnp.int32)
    own = iota((16, 256), 0) + y_ref[0] * 16
    held = (own & 31) * 8 + core_ref[0] * 4 + (own >> 5)
    pick_ref[...] = jnp.where(of_col * 4 + (iota((16, 256), 1) & 3) == held, 1.0, 0.0).astype(BF)


def out_kernel(x_ref, own_ref, other_ref, out_ref, wide):
    for n in range(4):
        wide[n] = x_ref[:, :, n * 128 : (n + 1) * 128].reshape(512, 128).astype(F32)
    pad = jnp.zeros((128 - WIDTH, 512), BF)
    total = jnp.zeros((128, 256), F32)
    for k in range(4):
        rows = []
        for t in range(4):
            tiles = [wide[n, pl.ds(k * 4 + t, 32, stride=16), :] for n in range(4)]
            rows.append(jnp.concatenate(tiles, axis=1).astype(BF))
        cut = slice(k * 512, (k + 1) * 512)
        w = jnp.concatenate([own_ref[:, cut], pad, other_ref[:, cut], pad], axis=0)
        total = total + lax.dot_general(
            jnp.concatenate(rows, axis=0), w, (((1,), (1,)), ((), ())), preferred_element_type=F32
        )
    total = total.astype(BF)
    for y in range(8):
        part = total[y * 16 : y * 16 + 16]
        out_ref[y, 0:16, :] = part[:, :128]
        out_ref[y, 16:32, :] = part[:, 128:]


def norm_kernel(part_ref, pick_ref, own_ref, other_ref, out_ref, hidden_ref):
    attended = part_ref[0].astype(F32)
    for i in range(1, 8):
        attended = attended + part_ref[i].astype(F32)
    attended = attended[:, :WIDTH]
    nt = (((1,), (1,)), ((), ()))
    pick = pick_ref[...]
    unit = (lax.broadcasted_iota(jnp.int32, (16, 128), 1) == 0).astype(F32).astype(BF)
    picked = lambda ref: lax.dot_general(pick, ref[:, :256], nt, preferred_element_type=F32)
    gains = lambda ref: lax.dot_general(unit, ref[:, 256:], nt, preferred_element_type=F32)
    hidden = attended + jnp.concatenate([picked(own_ref), picked(other_ref)], axis=0)
    gain = jnp.concatenate([gains(own_ref), gains(other_ref)], axis=0)
    squares = jnp.sum(hidden * hidden, axis=1, keepdims=True)
    squares = squares[0:16] + squares[16:32]
    none = jnp.zeros((32, 128 - WIDTH), F32)
    scaled = jnp.concatenate([hidden * gain, none], axis=1)
    lane = lax.broadcasted_iota(jnp.int32, (32, 128), 1)
    first = lax.broadcasted_iota(jnp.int32, (32, 128), 0) < 16
    high = squares.astype(BF).astype(F32)
    twice = lambda a: jnp.concatenate([a, a], axis=0)
    scaled = jnp.where(first & (lane == WIDTH), twice(high), scaled)
    scaled = jnp.where(first & (lane == WIDTH + 1), twice(squares - high), scaled).astype(BF)
    hidden_ref[...] = jnp.concatenate([hidden, none], axis=1)
    for i in range(32):
        out_ref[i] = scaled


def gate_kernel(xh_ref, xl_ref, full_ref, *refs):
    own_refs, other_refs, out_ref = refs[:4], refs[4:7], refs[7]
    lane = lax.broadcasted_iota(jnp.int32, (128, 128), 1)
    valid = lane < WIDTH
    none = jnp.zeros((128 - WIDTH, 384), BF)
    zero = jnp.zeros((128, 128), BF)
    held, squares = [], jnp.zeros((128, 1), F32)
    for r in range(4):
        x = 2 * (xh_ref[0] ^ (r >> 1)) + (xl_ref[0] ^ (r & 1))
        block = full_ref[pl.ds(x * 8, 8)]
        own = block[:, 0:16, :].reshape(128, 128)
        other = block[:, 16:32, :].reshape(128, 128)
        sums = jnp.where((lane == WIDTH) | (lane == WIDTH + 1), own.astype(F32), 0.0)
        squares = squares + jnp.sum(sums, axis=1, keepdims=True)
        both = [jnp.where(valid, own, zero), jnp.where(valid, other, zero)]
        held.append(jnp.concatenate(both, axis=1))
    for n in range(0, 2 * SIZE, 384):
        total = jnp.zeros((128, 384), F32)
        for r in range(4):
            k, at = divmod(r * 2 * SIZE + n, 4 * 384)
            both = [own_refs[r][:, n : n + 384], none, other_refs[k][:, at : at + 384], none]
            total = total + dot(held[r], jnp.concatenate(both, axis=0))
        out_ref[:, :, n : n + 384] = total.astype(BF).reshape(8, 16, 384)
    high = squares.astype(BF).astype(F32)
    last = jnp.where(lane == 0, high, jnp.where(lane == 1, squares - high, 0.0))
    out_ref[:, :, 1152:1280] = last.astype(BF).reshape(8, 16, 128)


def units_kernel(part_ref, out_ref):
    total = part_ref[0].astype(F32)
    for i in range(1, 8):
        total = total + part_ref[i].astype(F32)
    squares = total[:, 2 * SIZE : 2 * SIZE + 1] + total[:, 2 * SIZE + 1 : 2 * SIZE + 2]
    factor = lax.rsqrt(squares / D + norm_eps)
    gate = total[:, :SIZE] * factor
    up = total[:, SIZE : 2 * SIZE] * factor
    units = (gate * jax.nn.sigmoid(gate) * up).astype(BF)
    for i in range(8):
        out_ref[i] = units


def down_kernel(
    xh_ref, xl_ref, y_ref, own_ref, other_ref, w0, w1, w2, w3, hidden_ref, across_ref, place_ref, out_ref, total
):
    units = jnp.concatenate([own_ref[...].reshape(128, SIZE), other_ref[...].reshape(128, SIZE)], axis=0)
    place = place_ref[...]
    none = jnp.zeros((128 - WIDTH, SIZE), BF)
    nt = (((1,), (1,)), ((), ()))
    for r, w in enumerate((w0, w1, w2, w3)):
        wide = jnp.concatenate([w[:, w.shape[1] - SIZE :], none], axis=0)
        part = lax.dot_general(units, wide, nt, preferred_element_type=F32)
        if r == 0:
            total[...] = part
            at = pl.multiple_of(y_ref[0] * 16, 16)
            total[pl.ds(at, 16), :] += hidden_ref[0:16, :]
            total[pl.ds(128 + at, 16), :] += across_ref[...]
            part = total[...]
        rows = dot(place, part.astype(BF)).astype(BF)
        x = 2 * (xh_ref[0] ^ (r >> 1)) + (xl_ref[0] ^ (r & 1))
        out_ref[pl.ds(x * 8, 8)] = rows.reshape(8, 32, 128)


def swap(value, axis="c"):
    return lax.ppermute(value, axis, [(0, 1), (1, 0)])


def exchange(blocks, axes):
    return lax.all_to_all(blocks, axes, 0, 0, tiled=True)


def diagonal(value):
    return lax.ppermute(value, ("xh", "xl"), [(i, 3 - i) for i in range(4)])


def local(
    queries,
    new_latents,
    latent_cache,
    lengths,
    slot_of,
    value_maps,
    out_proj,
    residual,
    norm_gain,
    w_gate,
    w_up,
    w_down,
):
    xh, xl, core, tp = (lax.axis_index(a)[None].astype(jnp.int32) for a in ("xh", "xl", "c", "y"))

    blocks = call(
        attention_kernel,
        [SMEM, HBM, VMEM, HBM, HBM],
        shape((32, 16, 512)),
        [
            pltpu.VMEM((64, 576), BF),
            pltpu.VMEM((576, 512), BF),
            pltpu.VMEM((16, 512, 128), BF),
            pltpu.VMEM((4, 64, 128), F32),
            pltpu.VMEM((2, 8, 128), F32),
            pltpu.VMEM((16, 512), F32),
            pltpu.SemaphoreType.DMA((3,)),
        ],
        200_000_000,
        4_000_000,
        56,
    )(lengths, queries.reshape(64, -1), new_latents[0], latent_cache[0].T, value_maps)
    blocks, out_proj, slot_of, residual, norm_gain, w_gate, w_up, w_down = lax.optimization_barrier(
        (blocks, out_proj.T, slot_of, residual.T, norm_gain, w_gate, w_up, w_down.T)
    )
    rows = exchange(blocks, ("z", "xh", "xl"))
    gains = jnp.broadcast_to(norm_gain[:, None], (WIDTH, 128))
    carry, *ff = call(
        pack_kernel,
        [SMEM] * 2 + [VMEM] * 6,
        [shape((WIDTH, 2048 + 256 + 128))]
        + [shape((WIDTH, n * SIZE)) for n in (2, 3, 2, 2)],
        (),
        0,
        3_200_000,
    )(xh, xl, w_gate, w_up, w_down, out_proj, residual, gains)
    carry_other = swap(carry)
    ff = [ff[0], swap(ff[1], "xl"), swap(ff[2], "xh"), diagonal(ff[3])]
    rows, ff[0] = lax.optimization_barrier((rows, ff[0]))
    part = call(
        out_kernel,
        [VMEM] * 3,
        shape((8, 32, 128)),
        [pltpu.VMEM((4, 512, 128), F32)],
        1_000_000,
        100_000,
    )(rows, out_proj, carry_other)
    _, slot_of, w_down, tail, tail_other = lax.optimization_barrier(
        (part, slot_of, w_down, carry, carry_other)
    )
    tail, tail_other = tail[:, 2048:], tail_other[:, 2048:]
    pick, place = call(
        rows_kernel, [SMEM, SMEM, VMEM], [shape((16, 256)), shape((256, 256))], (), 0, 200_000
    )(core, tp, slot_of[None])
    down = call(
        pack_down_kernel, [SMEM, SMEM, VMEM], [shape((WIDTH, SIZE))] * 3, (), 0, 1_000_000
    )(xh, xl, w_down)
    _, _, ff = lax.optimization_barrier((pick, down, ff))
    joined = jnp.concatenate
    thirds = [
        joined([ff[0], ff[1][:, :384]], axis=1),
        joined([ff[1][:, 384 : 2 * SIZE], ff[2][:, :768]], axis=1),
        joined([ff[2][:, 768:], ff[3]], axis=1),
    ]
    part, ff, thirds, down, pick, tail, tail_other = lax.optimization_barrier(
        (exchange(part, "y"), ff, thirds, down, pick, tail, tail_other)
    )
    scaled, hidden = call(
        norm_kernel, [VMEM] * 4, [shape((32, 32, 128)), shape((32, 128), F32)], (), 0, 400_000
    )(part, pick, tail, tail_other)
    hidden, *thirds = lax.optimization_barrier((hidden, *thirds))
    ff_other = [swap(w) for w in thirds]
    part = call(
        gate_kernel, [SMEM] * 2 + [VMEM] * 8, shape((8, 16, 1280)), (), 300_000_000, 2_800_000
    )(xh, xl, exchange(scaled, ("xh", "xl", "y")), *ff, *ff_other)
    _, far, cross = lax.optimization_barrier((part, down[1], down[2]))
    part, far, cross = lax.optimization_barrier(
        (exchange(part, "z"), swap(far, "xh"), diagonal(cross))
    )
    units = call(units_kernel, [VMEM], shape((8, 16, SIZE)), (), 0, 500_000)(part)
    _, hidden = lax.optimization_barrier((units, hidden))
    units, across = lax.optimization_barrier((exchange(units, "z"), swap(hidden[16:])))
    down = (down[0], ff[1], far, cross)
    part = call(
        down_kernel,
        [SMEM] * 3 + [VMEM] * 9,
        shape((32, 32, 128)),
        [pltpu.VMEM((256, 128), F32)],
        200_000_000,
        1_600_000,
    )(xh, xl, tp, units, swap(units), *down, hidden, across, place)
    total = jnp.sum(exchange(part, ("xh", "xl", "y"))[:, :, :WIDTH].astype(F32), axis=0)
    return total.astype(BF)


def solution(mesh):
    fine = Mesh(mesh.devices.reshape(8, 2, 2, 2, 8), AXES)
    specs = (
        P(DP, None, "y", None),
        P(DP, None, None),
        P(DP, None, None),
        P(DP),
        P(),
        P("y", None, None),
        P("y", DP),
        P(None, DP),
        P(DP),
        P(DP, "y"),
        P(DP, "y"),
        P("y", DP),
    )
    return jax.shard_map(
        local, mesh=fine, in_specs=specs, out_specs=P("y", DP), check_vma=False
    )
```

```python
import jax
import jax.numpy as jnp
from jax import lax
from jax.experimental import pallas as pl
from jax.experimental.pallas import tpu as pltpu
from jax.sharding import Mesh
from jax.sharding import PartitionSpec as P

D = 7168
WIDTH = 112
SIZE = 576

score_scale = 192.0 ** (-0.5)
norm_eps = 1e-06

AXES = ("z", "xh", "xl", "c", "y")
DP = ("z", "xh", "xl", "c")
BF = jnp.bfloat16
F32 = jnp.float32
VMEM = pl.BlockSpec(memory_space=pltpu.VMEM)
SMEM = pl.BlockSpec(memory_space=pltpu.SMEM)
HBM = pl.BlockSpec(memory_space=pltpu.HBM)


def call(kernel, in_specs, outs, scratch=(), flops=0, moved=0, limit=24):
    many = isinstance(outs, (list, tuple))
    return pl.pallas_call(
        kernel,
        in_specs=in_specs,
        out_specs=[VMEM] * len(outs) if many else VMEM,
        out_shape=list(outs) if many else outs,
        scratch_shapes=list(scratch),
        compiler_params=pltpu.CompilerParams(vmem_limit_bytes=limit * 1024 * 1024),
        cost_estimate=pl.CostEstimate(flops=flops, bytes_accessed=moved, transcendentals=0),
    )


def shape(dims, dtype=BF):
    return jax.ShapeDtypeStruct(dims, dtype)


def dot(a, b):
    return jnp.dot(a, b, preferred_element_type=F32)


def attention_kernel(len_ref, q_ref, new_ref, cache_ref, maps_ref, out_ref, q_in, cache, maps, ctx, pairs, heads, sems):
    fetches = [
        pltpu.make_async_copy(src, dst, sems.at[i])
        for i, (src, dst) in enumerate(((q_ref, q_in), (cache_ref, cache), (maps_ref, maps)))
    ]
    for fetch in fetches:
        fetch.start()
    new = new_ref[...]
    nt = (((1,), (1,)), ((), ()))
    fetches[0].wait()
    q = q_in[...]
    fresh = lax.dot_general(q, new, nt, preferred_element_type=F32) * score_scale
    fetches[1].wait()
    score = dot(q, cache[...]) * score_scale
    keep = lax.broadcasted_iota(jnp.int32, score.shape, 1) < len_ref[0]
    step = lax.broadcasted_iota(jnp.int32, fresh.shape, 0) // 16
    keep_new = lax.broadcasted_iota(jnp.int32, fresh.shape, 1) <= step
    score = jnp.where(keep, score, -1e30)
    fresh = jnp.where(keep_new, fresh, -1e30)
    top = jnp.maximum(
        jnp.max(score, axis=1, keepdims=True), jnp.max(fresh, axis=1, keepdims=True)
    )
    weight = jnp.where(keep, jnp.exp(score - top), 0.0)
    weight_new = jnp.where(keep_new, jnp.exp(fresh - top), 0.0)
    total = jnp.sum(weight, axis=1, keepdims=True) + jnp.sum(weight_new, axis=1, keepdims=True)
    prob = (weight / total).astype(BF)
    prob_new = (weight_new / total).astype(BF)
    context = lax.dot_general(prob, cache[:512, :], nt, preferred_element_type=F32)
    context = (context + dot(prob_new, new[:, :512])).astype(BF).astype(F32)
    for n in range(4):
        ctx[n] = context[:, n * 128 : (n + 1) * 128]
    fetches[2].wait()
    for h in range(8):
        rows = jnp.concatenate([ctx[n, pl.ds(h, 8, stride=8), :] for n in range(4)], axis=1).astype(BF)
        pair = dot(rows, jnp.concatenate([maps[h], maps[h + 8]], axis=1))
        for i, head in enumerate((h, h + 8)):
            pairs[i] = pair[:, i * 128 : i * 128 + 128]
            k, place = head // 4, head % 4
            heads[k * 4 : k * 4 + 4, place * 128 : place * 128 + 128] = pairs[i, pl.ds(i, 4, stride=2), :]
    block = heads[...].astype(BF)
    for i in range(32):
        out_ref[i] = block


def target(xh_ref, xl_ref, r):
    return 2 * (xh_ref[0] ^ (r >> 1)) + (xl_ref[0] ^ (r & 1))


def pack_kernel(xh_ref, xl_ref, gate_ref, up_ref, down_ref, proj_ref, residual_ref, gain_ref, carry_ref, *outs):
    carry_ref[:, :2048] = proj_ref[...]
    carry_ref[:, 2048:2304] = residual_ref[...]
    carry_ref[:, 2304:] = gain_ref[...]
    for i in range(4):
        cut = slice(i * SIZE, (i + 1) * SIZE)
        block = jnp.concatenate([gate_ref[:, cut], up_ref[:, cut]], axis=1)
        for r, out_ref in enumerate(outs):

            @pl.when(target(xh_ref, xl_ref, r) == i)
            def _(out_ref=out_ref, block=block, down=down_ref[:, cut] if r == 1 else None):
                out_ref[:, : 2 * SIZE] = block
                if down is not None:
                    out_ref[:, 2 * SIZE :] = down


def pack_down_kernel(xh_ref, xl_ref, down_ref, *outs):
    for i in range(4):
        block = down_ref[:, i * SIZE : (i + 1) * SIZE]
        for r, out_ref in zip((0, 2, 3), outs):

            @pl.when(target(xh_ref, xl_ref, r) == i)
            def _(out_ref=out_ref, block=block):
                out_ref[...] = block


def rows_kernel(core_ref, y_ref, slot_ref, pick_ref, place_ref):
    iota = lambda dims, axis: lax.broadcasted_iota(jnp.int32, dims, axis)
    slot = slot_ref[...].astype(F32)
    col = iota((256, 256), 1)
    held = (col & 31) * 8 + (col >> 7) * 4 + ((col >> 5) & 3)
    spread = (iota((256, 64), 0) >> 2) == iota((256, 64), 1)
    of_row = jnp.sum(jnp.where(spread, slot, 0.0), axis=1, keepdims=True).astype(jnp.int32)
    place = (of_row * 4 + (iota((256, 256), 0) & 3)) == held
    place_ref[...] = jnp.where(place, 1.0, 0.0).astype(BF)
    across = jnp.where((iota((64, 256), 1) >> 2) == iota((64, 256), 0), 1.0, 0.0).astype(BF)
    of_col = dot(jnp.broadcast_to(slot, (16, 64)).astype(BF), across).astype(jnp.int32)
    own = iota((16, 256), 0) + y_ref[0] * 16
    held = (own & 31) * 8 + core_ref[0] * 4 + (own >> 5)
    pick_ref[...] = jnp.where(of_col * 4 + (iota((16, 256), 1) & 3) == held, 1.0, 0.0).astype(BF)


def out_kernel(x_ref, own_ref, other_ref, out_ref, wide):
    for n in range(4):
        wide[n] = x_ref[:, :, n * 128 : (n + 1) * 128].reshape(512, 128).astype(F32)
    pad = jnp.zeros((128 - WIDTH, 512), BF)
    total = jnp.zeros((128, 256), F32)
    for k in range(4):
        rows = []
        for t in range(4):
            tiles = [wide[n, pl.ds(k * 4 + t, 32, stride=16), :] for n in range(4)]
            rows.append(jnp.concatenate(tiles, axis=1).astype(BF))
        cut = slice(k * 512, (k + 1) * 512)
        w = jnp.concatenate([own_ref[:, cut], pad, other_ref[:, cut], pad], axis=0)
        total = total + lax.dot_general(
            jnp.concatenate(rows, axis=0), w, (((1,), (1,)), ((), ())), preferred_element_type=F32
        )
    total = total.astype(BF)
    for y in range(8):
        part = total[y * 16 : y * 16 + 16]
        out_ref[y, 0:16, :] = part[:, :128]
        out_ref[y, 16:32, :] = part[:, 128:]


def norm_kernel(part_ref, pick_ref, own_ref, other_ref, out_ref, hidden_ref):
    attended = part_ref[0].astype(F32)
    for i in range(1, 8):
        attended = attended + part_ref[i].astype(F32)
    attended = attended[:, :WIDTH]
    nt = (((1,), (1,)), ((), ()))
    pick = pick_ref[...]
    unit = (lax.broadcasted_iota(jnp.int32, (16, 128), 1) == 0).astype(F32).astype(BF)
    picked = lambda ref: lax.dot_general(pick, ref[:, :256], nt, preferred_element_type=F32)
    gains = lambda ref: lax.dot_general(unit, ref[:, 256:], nt, preferred_element_type=F32)
    hidden = attended + jnp.concatenate([picked(own_ref), picked(other_ref)], axis=0)
    gain = jnp.concatenate([gains(own_ref), gains(other_ref)], axis=0)
    squares = jnp.sum(hidden * hidden, axis=1, keepdims=True)
    squares = squares[0:16] + squares[16:32]
    none = jnp.zeros((32, 128 - WIDTH), F32)
    scaled = jnp.concatenate([hidden * gain, none], axis=1)
    lane = lax.broadcasted_iota(jnp.int32, (32, 128), 1)
    first = lax.broadcasted_iota(jnp.int32, (32, 128), 0) < 16
    high = squares.astype(BF).astype(F32)
    twice = lambda a: jnp.concatenate([a, a], axis=0)
    scaled = jnp.where(first & (lane == WIDTH), twice(high), scaled)
    scaled = jnp.where(first & (lane == WIDTH + 1), twice(squares - high), scaled).astype(BF)
    hidden_ref[...] = jnp.concatenate([hidden, none], axis=1)
    for i in range(32):
        out_ref[i] = scaled


def gate_kernel(xh_ref, xl_ref, full_ref, *refs):
    own_refs, other_refs, out_ref = refs[:4], refs[4:7], refs[7]
    lane = lax.broadcasted_iota(jnp.int32, (128, 128), 1)
    valid = lane < WIDTH
    none = jnp.zeros((128 - WIDTH, 384), BF)
    zero = jnp.zeros((128, 128), BF)
    held, squares = [], jnp.zeros((128, 1), F32)
    for r in range(4):
        x = 2 * (xh_ref[0] ^ (r >> 1)) + (xl_ref[0] ^ (r & 1))
        block = full_ref[pl.ds(x * 8, 8)]
        own = block[:, 0:16, :].reshape(128, 128)
        other = block[:, 16:32, :].reshape(128, 128)
        sums = jnp.where((lane == WIDTH) | (lane == WIDTH + 1), own.astype(F32), 0.0)
        squares = squares + jnp.sum(sums, axis=1, keepdims=True)
        both = [jnp.where(valid, own, zero), jnp.where(valid, other, zero)]
        held.append(jnp.concatenate(both, axis=1))
    for n in range(0, 2 * SIZE, 384):
        total = jnp.zeros((128, 384), F32)
        for r in range(4):
            k, at = divmod(r * 2 * SIZE + n, 4 * 384)
            both = [own_refs[r][:, n : n + 384], none, other_refs[k][:, at : at + 384], none]
            total = total + dot(held[r], jnp.concatenate(both, axis=0))
        out_ref[:, :, n : n + 384] = total.astype(BF).reshape(8, 16, 384)
    high = squares.astype(BF).astype(F32)
    last = jnp.where(lane == 0, high, jnp.where(lane == 1, squares - high, 0.0))
    out_ref[:, :, 1152:1280] = last.astype(BF).reshape(8, 16, 128)


def units_kernel(part_ref, out_ref):
    total = part_ref[0].astype(F32)
    for i in range(1, 8):
        total = total + part_ref[i].astype(F32)
    squares = total[:, 2 * SIZE : 2 * SIZE + 1] + total[:, 2 * SIZE + 1 : 2 * SIZE + 2]
    factor = lax.rsqrt(squares / D + norm_eps)
    gate = total[:, :SIZE] * factor
    up = total[:, SIZE : 2 * SIZE] * factor
    units = (gate * jax.nn.sigmoid(gate) * up).astype(BF)
    for i in range(16):
        out_ref[i] = units


def down_kernel(
    xh_ref, xl_ref, core_ref, y_ref, units_ref, w0, w1, w2, w3, hidden_ref, across_ref, place_ref, out_ref, total
):
    units = jnp.concatenate([units_ref[:, i].reshape(128, SIZE) for i in range(2)], axis=0)
    place = place_ref[...]
    none = jnp.zeros((128 - WIDTH, SIZE), BF)
    nt = (((1,), (1,)), ((), ()))
    for r, w in enumerate((w0, w1, w2, w3)):
        wide = jnp.concatenate([w[:, w.shape[1] - SIZE :], none], axis=0)
        part = lax.dot_general(units, wide, nt, preferred_element_type=F32)
        if r == 0:
            total[...] = part
            here = pl.multiple_of(core_ref[0] * 128 + y_ref[0] * 16, 16)
            total[pl.ds(here, 16), :] += hidden_ref[0:16, :]
            there = pl.multiple_of((1 - core_ref[0]) * 128 + y_ref[0] * 16, 16)
            total[pl.ds(there, 16), :] += across_ref[...]
            part = total[...]
        rows = dot(place, part.astype(BF)).astype(BF)
        x = 2 * (xh_ref[0] ^ (r >> 1)) + (xl_ref[0] ^ (r & 1))
        out_ref[pl.ds(x * 8, 8)] = rows.reshape(8, 32, 128)


def swap(value, axis="c"):
    return lax.ppermute(value, axis, [(0, 1), (1, 0)])


def exchange(blocks, axes):
    return lax.all_to_all(blocks, axes, 0, 0, tiled=True)


def diagonal(value):
    return lax.ppermute(value, ("xh", "xl"), [(i, 3 - i) for i in range(4)])


def local(
    queries,
    new_latents,
    latent_cache,
    lengths,
    slot_of,
    value_maps,
    out_proj,
    residual,
    norm_gain,
    w_gate,
    w_up,
    w_down,
):
    xh, xl, core, tp = (lax.axis_index(a)[None].astype(jnp.int32) for a in ("xh", "xl", "c", "y"))

    blocks = call(
        attention_kernel,
        [SMEM, HBM, VMEM, HBM, HBM],
        shape((32, 16, 512)),
        [
            pltpu.VMEM((64, 576), BF),
            pltpu.VMEM((576, 512), BF),
            pltpu.VMEM((16, 512, 128), BF),
            pltpu.VMEM((4, 64, 128), F32),
            pltpu.VMEM((2, 8, 128), F32),
            pltpu.VMEM((16, 512), F32),
            pltpu.SemaphoreType.DMA((3,)),
        ],
        200_000_000,
        4_000_000,
        56,
    )(lengths, queries.reshape(64, -1), new_latents[0], latent_cache[0].T, value_maps)
    blocks, out_proj, slot_of, residual, norm_gain, w_gate, w_up, w_down = lax.optimization_barrier(
        (blocks, out_proj.T, slot_of, residual.T, norm_gain, w_gate, w_up, w_down.T)
    )
    rows = exchange(blocks, ("z", "xh", "xl"))
    gains = jnp.broadcast_to(norm_gain[:, None], (WIDTH, 128))
    carry, *ff = call(
        pack_kernel,
        [SMEM] * 2 + [VMEM] * 6,
        [shape((WIDTH, 2048 + 256 + 128))]
        + [shape((WIDTH, n * SIZE)) for n in (2, 3, 2, 2)],
        (),
        0,
        3_200_000,
    )(xh, xl, w_gate, w_up, w_down, out_proj, residual, gains)
    carry_other = swap(carry)
    ff = [ff[0], swap(ff[1], "xl"), swap(ff[2], "xh"), diagonal(ff[3])]
    rows, ff[0] = lax.optimization_barrier((rows, ff[0]))
    part = call(
        out_kernel,
        [VMEM] * 3,
        shape((8, 32, 128)),
        [pltpu.VMEM((4, 512, 128), F32)],
        1_000_000,
        100_000,
    )(rows, out_proj, carry_other)
    _, slot_of, w_down, tail, tail_other = lax.optimization_barrier(
        (part, slot_of, w_down, carry, carry_other)
    )
    tail, tail_other = tail[:, 2048:], tail_other[:, 2048:]
    pick, place = call(
        rows_kernel, [SMEM, SMEM, VMEM], [shape((16, 256)), shape((256, 256))], (), 0, 200_000
    )(core, tp, slot_of[None])
    down = call(
        pack_down_kernel, [SMEM, SMEM, VMEM], [shape((WIDTH, SIZE))] * 3, (), 0, 1_000_000
    )(xh, xl, w_down)
    _, _, ff = lax.optimization_barrier((pick, down, ff))
    joined = jnp.concatenate
    thirds = [
        joined([ff[0], ff[1][:, :384]], axis=1),
        joined([ff[1][:, 384 : 2 * SIZE], ff[2][:, :768]], axis=1),
        joined([ff[2][:, 768:], ff[3]], axis=1),
    ]
    part, ff, thirds, down, pick, tail, tail_other = lax.optimization_barrier(
        (exchange(part, "y"), ff, thirds, down, pick, tail, tail_other)
    )
    scaled, hidden = call(
        norm_kernel, [VMEM] * 4, [shape((32, 32, 128)), shape((32, 128), F32)], (), 0, 400_000
    )(part, pick, tail, tail_other)
    hidden, *thirds = lax.optimization_barrier((hidden, *thirds))
    ff_other = [swap(w) for w in thirds]
    part = call(
        gate_kernel, [SMEM] * 2 + [VMEM] * 8, shape((8, 16, 1280)), (), 300_000_000, 2_800_000
    )(xh, xl, exchange(scaled, ("xh", "xl", "y")), *ff, *ff_other)
    _, hidden, far = lax.optimization_barrier((part, hidden, down[1]))
    part, far, across = lax.optimization_barrier(
        (exchange(part, "z"), swap(far, "xh"), swap(hidden[16:]))
    )
    units = call(units_kernel, [VMEM], shape((16, 16, SIZE)), (), 0, 500_000)(part)
    _, cross = lax.optimization_barrier((units, down[2]))
    units, cross = lax.optimization_barrier((exchange(units, ("z", "c")), diagonal(cross)))
    down = (down[0], ff[1], far, cross)
    part = call(
        down_kernel,
        [SMEM] * 4 + [VMEM] * 8,
        shape((32, 32, 128)),
        [pltpu.VMEM((256, 128), F32)],
        200_000_000,
        1_600_000,
    )(xh, xl, core, tp, units.reshape(8, 2, 16, SIZE), *down, hidden, across, place)
    total = jnp.sum(exchange(part, ("xh", "xl", "y"))[:, :, :WIDTH].astype(F32), axis=0)
    return total.astype(BF)


def solution(mesh):
    fine = Mesh(mesh.devices.reshape(8, 2, 2, 2, 8), AXES)
    specs = (
        P(DP, None, "y", None),
        P(DP, None, None),
        P(DP, None, None),
        P(DP),
        P(),
        P("y", None, None),
        P("y", DP),
        P(None, DP),
        P(DP),
        P(DP, "y"),
        P(DP, "y"),
        P("y", DP),
    )
    return jax.shard_map(
        local, mesh=fine, in_specs=specs, out_specs=P("y", DP), check_vma=False
    )
```

```python
import jax
import jax.numpy as jnp
from jax import lax
from jax.experimental import pallas as pl
from jax.experimental.pallas import tpu as pltpu
from jax.sharding import Mesh
from jax.sharding import PartitionSpec as P

D = 7168
WIDTH = 112
SIZE = 576

score_scale = 192.0 ** (-0.5)
norm_eps = 1e-06

AXES = ("z", "xh", "xl", "c", "y")
DP = ("z", "xh", "xl", "c")
BF = jnp.bfloat16
F32 = jnp.float32
VMEM = pl.BlockSpec(memory_space=pltpu.VMEM)
SMEM = pl.BlockSpec(memory_space=pltpu.SMEM)
HBM = pl.BlockSpec(memory_space=pltpu.HBM)


def call(kernel, in_specs, outs, scratch=(), flops=0, moved=0, limit=24):
    many = isinstance(outs, (list, tuple))
    return pl.pallas_call(
        kernel,
        in_specs=in_specs,
        out_specs=[VMEM] * len(outs) if many else VMEM,
        out_shape=list(outs) if many else outs,
        scratch_shapes=list(scratch),
        compiler_params=pltpu.CompilerParams(vmem_limit_bytes=limit * 1024 * 1024),
        cost_estimate=pl.CostEstimate(flops=flops, bytes_accessed=moved, transcendentals=0),
    )


def shape(dims, dtype=BF):
    return jax.ShapeDtypeStruct(dims, dtype)


def dot(a, b):
    return jnp.dot(a, b, preferred_element_type=F32)


def attention_kernel(len_ref, q_ref, new_ref, cache_ref, maps_ref, out_ref, q_in, cache, maps, ctx, pairs, heads, sems):
    fetches = [
        pltpu.make_async_copy(src, dst, sems.at[i])
        for i, (src, dst) in enumerate(((q_ref, q_in), (cache_ref, cache), (maps_ref, maps)))
    ]
    for fetch in fetches:
        fetch.start()
    new = new_ref[...]
    nt = (((1,), (1,)), ((), ()))
    fetches[0].wait()
    q = q_in[...]
    fresh = lax.dot_general(q, new, nt, preferred_element_type=F32) * score_scale
    fetches[1].wait()
    score = dot(q, cache[...]) * score_scale
    keep = lax.broadcasted_iota(jnp.int32, score.shape, 1) < len_ref[0]
    step = lax.broadcasted_iota(jnp.int32, fresh.shape, 0) // 16
    keep_new = lax.broadcasted_iota(jnp.int32, fresh.shape, 1) <= step
    score = jnp.where(keep, score, -1e30)
    fresh = jnp.where(keep_new, fresh, -1e30)
    top = jnp.maximum(
        jnp.max(score, axis=1, keepdims=True), jnp.max(fresh, axis=1, keepdims=True)
    )
    weight = jnp.where(keep, jnp.exp(score - top), 0.0)
    weight_new = jnp.where(keep_new, jnp.exp(fresh - top), 0.0)
    total = jnp.sum(weight, axis=1, keepdims=True) + jnp.sum(weight_new, axis=1, keepdims=True)
    prob = (weight / total).astype(BF)
    prob_new = (weight_new / total).astype(BF)
    context = lax.dot_general(prob, cache[:512, :], nt, preferred_element_type=F32)
    context = (context + dot(prob_new, new[:, :512])).astype(BF).astype(F32)
    for n in range(4):
        ctx[n] = context[:, n * 128 : (n + 1) * 128]
    fetches[2].wait()
    for h in range(8):
        rows = jnp.concatenate([ctx[n, pl.ds(h, 8, stride=8), :] for n in range(4)], axis=1).astype(BF)
        pair = dot(rows, jnp.concatenate([maps[h], maps[h + 8]], axis=1))
        for i, head in enumerate((h, h + 8)):
            pairs[i] = pair[:, i * 128 : i * 128 + 128]
            k, place = head // 4, head % 4
            heads[k * 4 : k * 4 + 4, place * 128 : place * 128 + 128] = pairs[i, pl.ds(i, 4, stride=2), :]
    block = heads[...].astype(BF)
    for i in range(32):
        out_ref[i] = block


def target(xh_ref, xl_ref, r):
    return 2 * (xh_ref[0] ^ (r >> 1)) + (xl_ref[0] ^ (r & 1))


def pack_kernel(xh_ref, xl_ref, gate_ref, up_ref, down_ref, proj_ref, residual_ref, gain_ref, carry_ref, *outs):
    carry_ref[:, :2048] = proj_ref[...]
    carry_ref[:, 2048:2304] = residual_ref[...]
    carry_ref[:, 2304:] = gain_ref[...]
    for i in range(4):
        cut = slice(i * SIZE, (i + 1) * SIZE)
        block = jnp.concatenate([gate_ref[:, cut], up_ref[:, cut]], axis=1)
        for r, out_ref in enumerate(outs):

            @pl.when(target(xh_ref, xl_ref, r) == i)
            def _(out_ref=out_ref, block=block, down=down_ref[:, cut] if r == 1 else None):
                out_ref[:, : 2 * SIZE] = block
                if down is not None:
                    out_ref[:, 2 * SIZE :] = down


def pack_down_kernel(xh_ref, xl_ref, down_ref, *outs):
    for i in range(4):
        block = down_ref[:, i * SIZE : (i + 1) * SIZE]
        for r, out_ref in zip((0, 2, 3), outs):

            @pl.when(target(xh_ref, xl_ref, r) == i)
            def _(out_ref=out_ref, block=block):
                out_ref[...] = block


def rows_kernel(core_ref, y_ref, slot_ref, pick_ref, place_ref):
    iota = lambda dims, axis: lax.broadcasted_iota(jnp.int32, dims, axis)
    slot = slot_ref[...].astype(F32)
    col = iota((256, 256), 1)
    held = (col & 31) * 8 + (col >> 7) * 4 + ((col >> 5) & 3)
    spread = (iota((256, 64), 0) >> 2) == iota((256, 64), 1)
    of_row = jnp.sum(jnp.where(spread, slot, 0.0), axis=1, keepdims=True).astype(jnp.int32)
    place = (of_row * 4 + (iota((256, 256), 0) & 3)) == held
    place_ref[...] = jnp.where(place, 1.0, 0.0).astype(BF)
    across = jnp.where((iota((64, 256), 1) >> 2) == iota((64, 256), 0), 1.0, 0.0).astype(BF)
    of_col = dot(jnp.broadcast_to(slot, (16, 64)).astype(BF), across).astype(jnp.int32)
    own = iota((16, 256), 0) + y_ref[0] * 16
    held = (own & 31) * 8 + core_ref[0] * 4 + (own >> 5)
    pick_ref[...] = jnp.where(of_col * 4 + (iota((16, 256), 1) & 3) == held, 1.0, 0.0).astype(BF)


def out_kernel(x_ref, own_ref, other_ref, out_ref, wide):
    for n in range(4):
        wide[n] = x_ref[:, :, n * 128 : (n + 1) * 128].reshape(512, 128).astype(F32)
    pad = jnp.zeros((128 - WIDTH, 512), BF)
    total = jnp.zeros((128, 256), F32)
    for k in range(4):
        rows = []
        for t in range(4):
            tiles = [wide[n, pl.ds(k * 4 + t, 32, stride=16), :] for n in range(4)]
            rows.append(jnp.concatenate(tiles, axis=1).astype(BF))
        cut = slice(k * 512, (k + 1) * 512)
        w = jnp.concatenate([own_ref[:, cut], pad, other_ref[:, cut], pad], axis=0)
        total = total + lax.dot_general(
            jnp.concatenate(rows, axis=0), w, (((1,), (1,)), ((), ())), preferred_element_type=F32
        )
    total = total.astype(BF)
    for y in range(8):
        part = total[y * 16 : y * 16 + 16]
        out_ref[y, 0:16, :] = part[:, :128]
        out_ref[y, 16:32, :] = part[:, 128:]


def norm_kernel(part_ref, pick_ref, own_ref, other_ref, out_ref, hidden_ref):
    attended = part_ref[0].astype(F32)
    for i in range(1, 8):
        attended = attended + part_ref[i].astype(F32)
    attended = attended[:, :WIDTH]
    nt = (((1,), (1,)), ((), ()))
    pick = pick_ref[...]
    unit = (lax.broadcasted_iota(jnp.int32, (16, 128), 1) == 0).astype(F32).astype(BF)
    picked = lambda ref: lax.dot_general(pick, ref[:, :256], nt, preferred_element_type=F32)
    gains = lambda ref: lax.dot_general(unit, ref[:, 256:], nt, preferred_element_type=F32)
    hidden = attended + jnp.concatenate([picked(own_ref), picked(other_ref)], axis=0)
    gain = jnp.concatenate([gains(own_ref), gains(other_ref)], axis=0)
    squares = jnp.sum(hidden * hidden, axis=1, keepdims=True)
    squares = squares[0:16] + squares[16:32]
    none = jnp.zeros((32, 128 - WIDTH), F32)
    scaled = jnp.concatenate([hidden * gain, none], axis=1)
    lane = lax.broadcasted_iota(jnp.int32, (32, 128), 1)
    first = lax.broadcasted_iota(jnp.int32, (32, 128), 0) < 16
    high = squares.astype(BF).astype(F32)
    twice = lambda a: jnp.concatenate([a, a], axis=0)
    scaled = jnp.where(first & (lane == WIDTH), twice(high), scaled)
    scaled = jnp.where(first & (lane == WIDTH + 1), twice(squares - high), scaled).astype(BF)
    hidden_ref[...] = jnp.concatenate([hidden, none], axis=1)
    for i in range(32):
        out_ref[i] = scaled


def gate_kernel(xh_ref, xl_ref, full_ref, *refs):
    own_refs, other_refs, out_ref = refs[:4], refs[4:7], refs[7]
    lane = lax.broadcasted_iota(jnp.int32, (128, 128), 1)
    valid = lane < WIDTH
    none = jnp.zeros((128 - WIDTH, 384), BF)
    zero = jnp.zeros((128, 128), BF)
    held, squares = [], jnp.zeros((128, 1), F32)
    for r in range(4):
        x = 2 * (xh_ref[0] ^ (r >> 1)) + (xl_ref[0] ^ (r & 1))
        block = full_ref[pl.ds(x * 8, 8)]
        own = block[:, 0:16, :].reshape(128, 128)
        other = block[:, 16:32, :].reshape(128, 128)
        sums = jnp.where((lane == WIDTH) | (lane == WIDTH + 1), own.astype(F32), 0.0)
        squares = squares + jnp.sum(sums, axis=1, keepdims=True)
        both = [jnp.where(valid, own, zero), jnp.where(valid, other, zero)]
        held.append(jnp.concatenate(both, axis=1))
    for n in range(0, 2 * SIZE, 384):
        total = jnp.zeros((128, 384), F32)
        for r in range(4):
            k, at = divmod(r * 2 * SIZE + n, 4 * 384)
            both = [own_refs[r][:, n : n + 384], none, other_refs[k][:, at : at + 384], none]
            total = total + dot(held[r], jnp.concatenate(both, axis=0))
        out_ref[:, :, n : n + 384] = total.astype(BF).reshape(8, 16, 384)
    high = squares.astype(BF).astype(F32)
    last = jnp.where(lane == 0, high, jnp.where(lane == 1, squares - high, 0.0))
    out_ref[:, :, 1152:1280] = last.astype(BF).reshape(8, 16, 128)


def units_kernel(part_ref, out_ref):
    total = part_ref[0].astype(F32)
    for i in range(1, 8):
        total = total + part_ref[i].astype(F32)
    squares = total[:, 2 * SIZE : 2 * SIZE + 1] + total[:, 2 * SIZE + 1 : 2 * SIZE + 2]
    factor = lax.rsqrt(squares / D + norm_eps)
    gate = total[:, :SIZE] * factor
    up = total[:, SIZE : 2 * SIZE] * factor
    units = (gate * jax.nn.sigmoid(gate) * up).astype(BF)
    for i in range(16):
        out_ref[i] = units


def down_kernel(
    xh_ref, xl_ref, core_ref, y_ref, units_ref, w0, w1, w2, w3, hidden_ref, across_ref, place_ref, out_ref, total
):
    units = jnp.concatenate([units_ref[:, i].reshape(128, SIZE) for i in range(2)], axis=0)
    place = place_ref[...]
    none = jnp.zeros((128 - WIDTH, SIZE), BF)
    nt = (((1,), (1,)), ((), ()))
    for r, w in enumerate((w0, w1, w2, w3)):
        wide = jnp.concatenate([w[:, w.shape[1] - SIZE :], none], axis=0)
        part = lax.dot_general(units, wide, nt, preferred_element_type=F32)
        if r == 0:
            total[...] = part
            here = pl.multiple_of(core_ref[0] * 128 + y_ref[0] * 16, 16)
            total[pl.ds(here, 16), :] += hidden_ref[0:16, :]
            there = pl.multiple_of((1 - core_ref[0]) * 128 + y_ref[0] * 16, 16)
            total[pl.ds(there, 16), :] += across_ref[...]
            part = total[...]
        rows = dot(place, part.astype(BF)).astype(BF)
        x = 2 * (xh_ref[0] ^ (r >> 1)) + (xl_ref[0] ^ (r & 1))
        out_ref[pl.ds(x * 8, 8)] = rows.reshape(8, 32, 128)


def swap(value, axis="c"):
    return lax.ppermute(value, axis, [(0, 1), (1, 0)])


def exchange(blocks, axes):
    return lax.all_to_all(blocks, axes, 0, 0, tiled=True)


def diagonal(value):
    return lax.ppermute(value, ("xh", "xl"), [(i, 3 - i) for i in range(4)])


def local(
    queries,
    new_latents,
    latent_cache,
    lengths,
    slot_of,
    value_maps,
    out_proj,
    residual,
    norm_gain,
    w_gate,
    w_up,
    w_down,
):
    xh, xl, core, tp = (lax.axis_index(a)[None].astype(jnp.int32) for a in ("xh", "xl", "c", "y"))

    blocks = call(
        attention_kernel,
        [SMEM, HBM, VMEM, HBM, HBM],
        shape((32, 16, 512)),
        [
            pltpu.VMEM((64, 576), BF),
            pltpu.VMEM((576, 512), BF),
            pltpu.VMEM((16, 512, 128), BF),
            pltpu.VMEM((4, 64, 128), F32),
            pltpu.VMEM((2, 8, 128), F32),
            pltpu.VMEM((16, 512), F32),
            pltpu.SemaphoreType.DMA((3,)),
        ],
        200_000_000,
        4_000_000,
        56,
    )(lengths, queries.reshape(64, -1), new_latents[0], latent_cache[0].T, value_maps)
    blocks, out_proj, slot_of, residual, norm_gain, w_gate, w_up, w_down = lax.optimization_barrier(
        (blocks, out_proj.T, slot_of, residual.T, norm_gain, w_gate, w_up, w_down.T)
    )
    rows = exchange(blocks, ("z", "xh", "xl"))
    gains = jnp.broadcast_to(norm_gain[:, None], (WIDTH, 128))
    carry, *ff = call(
        pack_kernel,
        [SMEM] * 2 + [VMEM] * 6,
        [shape((WIDTH, 2048 + 256 + 128))]
        + [shape((WIDTH, n * SIZE)) for n in (2, 3, 2, 2)],
        (),
        0,
        3_200_000,
    )(xh, xl, w_gate, w_up, w_down, out_proj, residual, gains)
    carry_other = swap(carry)
    far = swap(ff[2], "xh")
    cross = diagonal(ff[3])
    ff = [ff[0], swap(ff[1], "xl"), far, cross]
    rows, ff[0] = lax.optimization_barrier((rows, ff[0]))
    part = call(
        out_kernel,
        [VMEM] * 3,
        shape((8, 32, 128)),
        [pltpu.VMEM((4, 512, 128), F32)],
        1_000_000,
        100_000,
    )(rows, out_proj, carry_other)
    _, slot_of, w_down, tail, tail_other = lax.optimization_barrier(
        (part, slot_of, w_down, carry, carry_other)
    )
    tail, tail_other = tail[:, 2048:], tail_other[:, 2048:]
    pick, place = call(
        rows_kernel, [SMEM, SMEM, VMEM], [shape((16, 256)), shape((256, 256))], (), 0, 200_000
    )(core, tp, slot_of[None])
    down = call(
        pack_down_kernel, [SMEM, SMEM, VMEM], [shape((WIDTH, SIZE))] * 3, (), 0, 1_000_000
    )(xh, xl, w_down)
    *ff, _, _ = lax.optimization_barrier((*ff[::-1], pick, down))
    ff = ff[::-1]
    joined = jnp.concatenate
    thirds = [
        joined([ff[0], ff[1][:, :384]], axis=1),
        joined([ff[1][:, 384 : 2 * SIZE], ff[2][:, :768]], axis=1),
        joined([ff[2][:, 768:], ff[3]], axis=1),
    ]
    part, ff, thirds, down, pick, tail, tail_other = lax.optimization_barrier(
        (exchange(part, "y"), ff, thirds, down, pick, tail, tail_other)
    )
    scaled, hidden = call(
        norm_kernel, [VMEM] * 4, [shape((32, 32, 128)), shape((32, 128), F32)], (), 0, 400_000
    )(part, pick, tail, tail_other)
    hidden, *thirds = lax.optimization_barrier((hidden, *thirds))
    ff_other = [swap(w) for w in thirds]
    part = call(
        gate_kernel, [SMEM] * 2 + [VMEM] * 8, shape((8, 16, 1280)), (), 300_000_000, 2_800_000
    )(xh, xl, exchange(scaled, ("xh", "xl", "y")), *ff, *ff_other)
    _, hidden, far = lax.optimization_barrier((part, hidden, down[1]))
    part, far, across = lax.optimization_barrier(
        (exchange(part, "z"), swap(far, "xh"), swap(hidden[16:]))
    )
    units = call(units_kernel, [VMEM], shape((16, 16, SIZE)), (), 0, 500_000)(part)
    _, cross = lax.optimization_barrier((units, down[2]))
    units, cross = lax.optimization_barrier((exchange(units, ("z", "c")), diagonal(cross)))
    down = (down[0], ff[1], far, cross)
    part = call(
        down_kernel,
        [SMEM] * 4 + [VMEM] * 8,
        shape((32, 32, 128)),
        [pltpu.VMEM((256, 128), F32)],
        200_000_000,
        1_600_000,
    )(xh, xl, core, tp, units.reshape(8, 2, 16, SIZE), *down, hidden, across, place)
    total = jnp.sum(exchange(part, ("xh", "xl", "y"))[:, :, :WIDTH].astype(F32), axis=0)
    return total.astype(BF)


def solution(mesh):
    fine = Mesh(mesh.devices.reshape(8, 2, 2, 2, 8), AXES)
    specs = (
        P(DP, None, "y", None),
        P(DP, None, None),
        P(DP, None, None),
        P(DP),
        P(),
        P("y", None, None),
        P("y", DP),
        P(None, DP),
        P(DP),
        P(DP, "y"),
        P(DP, "y"),
        P("y", DP),
    )
    return jax.shard_map(
        local, mesh=fine, in_specs=specs, out_specs=P("y", DP), check_vma=False
    )
```
